512 devices in a mesh: sec: 4 (over x), cell: 64 (over z, y), dir: 2 (over core).
Axes of the slice: x: 4, y: 4, z: 16, core: 2. Of those that a mesh axis runs over, the one named last changes fastest.
Arguments:
- volume_field: bfloat16 [49152, 256], P(('sec', 'cell')), may hold values from -6 to 6
- contrast_id: int32 [49152, 256], P(('sec', 'cell')), may hold values from 0 to 15
- contrast: float32 [16], replicated, may hold values from 0.1 to 2
- near_index: int32 [49152, 27], P(('sec', 'cell', 'dir')), may hold values from -1 to 287, as said below
- near_blocks: bfloat16 [27, 256, 256], replicated, may hold values from -0.078125 to 0.078125
- vol_radiation: bfloat16 [256, 256], P(None, 'dir'), may hold values from -0.375 to 0.375
- surf_radiation: bfloat16 [128, 256], P(None, 'dir'), may hold values from -0.5 to 0.5
- vol_receive: bfloat16 [256, 256], replicated, may hold values from -0.375 to 0.375
- surf_receive: bfloat16 [256, 128], replicated, may hold values from -0.375 to 0.375
- surface_current: bfloat16 [32768, 128], P(('sec', 'cell')), may hold values from -6 to 6
- surf_host: int32 [32768], P(('sec', 'cell')), may hold values from 0 to 191
- leaf_out: bfloat16 [192, 256], P(None, 'dir'), may hold values from -0.4375 to 0.4375
- leaf_in: bfloat16 [192, 256], P(None, 'dir'), may hold values from -4 to 4
- level_tables: float32 [4, 8, 256], P(None, None, 'dir'), may hold values from -4 to 4
- sv_blocks: bfloat16 [4, 128, 256], replicated, may hold values from -0.375 to 0.375
- pair_table: int32 [65536, 4, 3], P(('sec', 'cell', 'dir')), may hold values from -1 to 95, as said below
Outputs:
- volume_image: float32 [49152, 256], P(('sec', 'cell', 'dir'))
- surface_image: float32 [32768, 128], P(('sec', 'cell', 'dir'))
The draws below stay inside these ranges and needn't reach their ends.
Inputs may be any that keep to these rules, and one draw needn't show every extreme that they name: `near_index`: entry w of row r names the leaf cell 192 * (r // 192) + w - 48, in a window that reaches 48 cells into each neighbouring coarse cell; -1 marks a missing block; the middle slot names the cell itself. `pair_table`: per slot: surface row among the core's 128 / 2 (-1 for an empty slot), volume row among the target core's 192 / 2, block kind. Live slots come first in each row; a row holds up to 4 pairs, and in every draw some target core receives 4 pairs from every core of its section.
All inputs are finite; a program needn't handle non-finite values.
Results may differ from the reference program's by a relative error of at most 0.0036.
Values may be sent and summed in bfloat16 or wider, within the bound.
A program may use at most 64 MiB of HBM per device.

```python
import math
import jax
import jax.numpy as jnp
from jax import lax

VX = 256
KW = 256
SB = 128
NN = 27
NT = 4
NMAT = 16
LEVELS = 4
CAP = 4
LC = 192
LS = 128
HW = 48
NGRP = 256
CORES = 512
PEERS = 128
NCELLS = 49152
NSURF = 32768
N_CELL = 64
N_DIR = 2


def draw_near_index(key, part):
    key_far, key_mid, key_gap = jax.random.split(jax.random.fold_in(key, 11), 3)
    slot_ids = jnp.arange(NN, dtype=jnp.int32)
    step_x = slot_ids // 9 - 1
    step_y = slot_ids // 3 % 3 - 1
    step_z = slot_ids % 3 - 1
    far_step = jax.random.randint(key_far, (NCELLS, NN), HW // 2, HW + 1)
    mid_step = jax.random.randint(key_mid, (NCELLS, NN), 2, 9)
    offset = jnp.clip(step_x[None, :] * far_step + step_y[None, :] * mid_step + step_z[None, :], -HW, HW)
    position = jnp.arange(NCELLS, dtype=jnp.int32) % LC
    window = position[:, None] + HW + offset
    missing = (jax.random.randint(key_gap, (NCELLS, NN), 0, 8) == 0) & (slot_ids != NN // 2)[None, :]
    return jnp.where(missing, -1, window).astype(jnp.int32)


def draw_pair_table(key, part):
    keys = jax.random.split(jax.random.fold_in(key, 23), 5)
    base_count = jax.random.randint(keys[0], (CORES, PEERS), 0, CAP // 2 + 1)
    order = jax.random.permutation(keys[1], PEERS)
    heavy = order < max(1, PEERS // 16)
    counts = jnp.where(heavy[None, :], CAP, base_count)
    live = jnp.arange(CAP, dtype=jnp.int32)[None, None, :] < counts[:, :, None]
    surf_slot = jax.random.randint(keys[2], (CORES, PEERS, CAP), 0, LS // 2)
    surf_slot = jnp.where(live, surf_slot, -1)
    cell_slot = jax.random.randint(keys[3], (CORES, PEERS, CAP), 0, LC // 2)
    kind_slot = jax.random.randint(keys[4], (CORES, PEERS, CAP), 0, NT)
    return jnp.stack([surf_slot, cell_slot, kind_slot], axis=-1).reshape(CORES * PEERS, CAP, 3).astype(jnp.int32)


def touch_ends(array, own_key, smallest, high):
    extent = array.shape
    index_at = [jax.random.randint(jax.random.fold_in(own_key, axis), (), 0, extent[axis]) for axis in range(len(extent))]
    array = array.at[tuple(index_at)].set(smallest)
    longest = extent.index(max(extent))
    index_at[longest] = (index_at[longest] + 1) % extent[longest]
    return array.at[tuple(index_at)].set(high)


def steps_of(rng, dims, pieces, smallest, largest):
    def one(axis_at, shards_of):
        steps = jax.random.uniform(jax.random.fold_in(jax.random.fold_in(rng, 6), axis_at), (shards_of,), jnp.float32, smallest / len(pieces), largest / len(pieces))
        return jnp.repeat(jnp.exp(steps), dims[axis_at] // shards_of).reshape((-1,) + (1,) * (len(dims) - axis_at - 1))

    level = one(*pieces[0])
    for cut in pieces[1:]:
        level = level * one(*cut)
    return level


def normal_values(key, shape, spread, limit, pieces=(), kind=jnp.bfloat16):
    values = spread * jax.random.normal(key, shape, jnp.float32)
    if pieces:
        values = values * steps_of(key, shape, pieces, -0.22, 0.18)
    return jnp.clip(values, -limit, limit).astype(kind)


def setup_inputs(seed: int = 0) -> dict:
    arg_keys = jax.random.split(jax.random.key(seed), 17)
    return {
        "volume_field": normal_values(arg_keys[0], (NCELLS, VX), 1.0, 6.0, ((0, 256),)),
        "contrast_id": touch_ends(jax.random.randint(arg_keys[1], (NCELLS, VX), 0, NMAT), jax.random.fold_in(arg_keys[1], 1), 0, NMAT - 1).astype(jnp.int32),
        "contrast": jnp.clip(jnp.exp(jax.random.uniform(arg_keys[2], (NMAT,), jnp.float32, math.log(0.1), math.log(2.0))), 0.1, 2.0),
        "near_index": draw_near_index(jax.random.fold_in(arg_keys[16], 71), 0),
        "near_blocks": normal_values(arg_keys[4], (NN, VX, VX), (NN * VX) ** -0.5, 0.078125),
        "vol_radiation": normal_values(arg_keys[5], (VX, KW), VX ** -0.5, 0.375, ((1, 2),)),
        "surf_radiation": normal_values(arg_keys[6], (SB, KW), SB ** -0.5, 0.5, ((1, 2),)),
        "vol_receive": normal_values(arg_keys[7], (KW, VX), KW ** -0.5, 0.375),
        "surf_receive": normal_values(arg_keys[8], (KW, SB), KW ** -0.5, 0.375),
        "surface_current": normal_values(arg_keys[9], (NSURF, SB), 1.0, 6.0, ((0, 256),)),
        "surf_host": touch_ends(jax.random.randint(arg_keys[10], (NSURF,), 0, LC), jax.random.fold_in(arg_keys[10], 1), 0, LC - 1).astype(jnp.int32),
        "leaf_out": normal_values(arg_keys[11], (LC, KW), LC ** -0.5, 0.4375, ((1, 2),)),
        "leaf_in": normal_values(arg_keys[12], (LC, KW), 1.0, 4.0, ((1, 2),)),
        "level_tables": normal_values(arg_keys[13], (LEVELS, 8, KW), 0.8, 4.0, ((2, 2),), jnp.float32),
        "sv_blocks": normal_values(arg_keys[14], (NT, SB, VX), VX ** -0.5, 0.375),
        "pair_table": draw_pair_table(jax.random.fold_in(arg_keys[16], 71), 0),
    }


def level_terms(upward, tables, level_id):
    cell_total = upward.shape[0]
    padded = jnp.pad(upward, ((3, 3), (0, 0)))
    parity = (jnp.arange(cell_total, dtype=jnp.int32) % 2)[:, None]

    def offset_rows(offset):
        return padded[3 + offset:3 + offset + cell_total]

    result = jnp.where(parity == 1, tables[level_id, 0] * offset_rows(-3), 0.0)
    result = result + tables[level_id, 1] * offset_rows(-2)
    result = result + tables[level_id, 2] * offset_rows(2)
    result = result + jnp.where(parity == 0, tables[level_id, 3] * offset_rows(3), 0.0)
    return result


def coarse_tree(coarse_all, tables):
    levels = tables.shape[0]
    upward = [coarse_all]
    for level_id in range(levels - 1):
        current = upward[-1]
        upward.append(tables[level_id, 4] * current[0::2] + tables[level_id, 5] * current[1::2])
    translated = [level_terms(upward[level_id], tables, level_id) for level_id in range(levels)]
    downward = translated[-1]
    for level_id in range(levels - 2, -1, -1):
        cell_total = translated[level_id].shape[0]
        parity = (jnp.arange(cell_total, dtype=jnp.int32) % 2)[:, None]
        shifted = jnp.where(parity == 1, tables[level_id, 7], tables[level_id, 6])
        downward = translated[level_id] + shifted * jnp.repeat(downward, 2, axis=0)
    return downward


def reference(volume_field, contrast_id, contrast, near_index, near_blocks, vol_radiation, surf_radiation, vol_receive, surf_receive, surface_current, surf_host, leaf_out, leaf_in, level_tables, sv_blocks, pair_table):
    contrast_map = jnp.zeros(volume_field.shape, jnp.float32)
    for material in range(NMAT):
        contrast_map = contrast_map + jnp.where(contrast_id == material, contrast[material], 0.0)
    weighted = (volume_field.astype(jnp.float32) * contrast_map).astype(jnp.bfloat16)

    stacked = near_blocks.reshape(NN * VX, VX)

    def near_group(group_id):
        slots_here = lax.dynamic_slice_in_dim(near_index, group_id * LC, LC, 0)
        global_ids = group_id * LC + slots_here - HW
        is_live = (slots_here >= 0) & (global_ids >= 0) & (global_ids < NCELLS)
        safe_ids = jnp.where(is_live, global_ids, 0).astype(jnp.int32)
        row_data = jnp.take(weighted, safe_ids.reshape(-1), axis=0).reshape(LC, NN, VX)
        row_data = jnp.where(is_live[:, :, None], row_data, jnp.zeros((), row_data.dtype))
        return jnp.dot(row_data.reshape(LC, NN * VX), stacked, preferred_element_type=jnp.float32)

    near_part = lax.map(near_group, jnp.arange(NGRP, dtype=jnp.int32)).reshape(NCELLS, VX)

    host_ids = ((jnp.arange(NSURF, dtype=jnp.int32) // LS) * LC + surf_host).astype(jnp.int32)
    outgoing = jnp.dot(weighted, vol_radiation, preferred_element_type=jnp.float32)
    surf_waves = jnp.dot(surface_current, surf_radiation, preferred_element_type=jnp.float32)
    outgoing = outgoing + jax.ops.segment_sum(surf_waves, host_ids, num_segments=NCELLS)
    coarse_out = jnp.sum(outgoing.reshape(NGRP, LC, KW) * leaf_out.astype(jnp.float32)[None], axis=1)

    downward = coarse_tree(coarse_out, level_tables)
    incoming = (leaf_in.astype(jnp.float32)[None] * downward[:, None, :]).reshape(NCELLS, KW).astype(jnp.bfloat16)
    far_volume = jnp.dot(incoming, vol_receive, preferred_element_type=jnp.float32)
    far_surface = jnp.dot(jnp.take(incoming, host_ids, axis=0), surf_receive, preferred_element_type=jnp.float32)

    slots_all = pair_table.reshape(CORES, PEERS, CAP, 3)
    source = jnp.arange(CORES, dtype=jnp.int32)[:, None, None]
    target = jnp.arange(PEERS, dtype=jnp.int32)[None, :, None]
    group_ids = source // N_DIR
    source_core = source % N_DIR
    section = group_ids // N_CELL
    target_group = section * N_CELL + target // N_DIR
    target_core = target % N_DIR
    surf_slot = slots_all[..., 0]
    is_live = (surf_slot >= 0).reshape(-1)
    surf_ids = jnp.where(surf_slot >= 0, group_ids * LS + source_core * (LS // 2) + surf_slot, 0).reshape(-1).astype(jnp.int32)
    vol_ids = (target_group * LC + target_core * (LC // 2) + slots_all[..., 1]).reshape(-1).astype(jnp.int32)
    kind_ids = slots_all[..., 2].reshape(-1)

    coupled_volume = jnp.zeros((NCELLS, VX), jnp.float32)
    coupled_surface = jnp.zeros((NSURF, SB), jnp.float32)
    for kind_id in range(NT):
        in_use = (is_live & (kind_ids == kind_id))[:, None]
        coupling = sv_blocks[kind_id]
        pushed_all = jnp.dot(surface_current, coupling, preferred_element_type=jnp.float32)
        pushed = jnp.where(in_use, jnp.take(pushed_all, surf_ids, axis=0), 0.0)
        coupled_volume = coupled_volume + jax.ops.segment_sum(pushed, vol_ids, num_segments=NCELLS)
        pulled_all = jnp.dot(weighted, coupling.T, preferred_element_type=jnp.float32)
        replies = lax.optimization_barrier(jnp.take(pulled_all, vol_ids, axis=0).astype(jnp.bfloat16)).astype(jnp.float32)
        replies = jnp.where(in_use, replies, 0.0)
        coupled_surface = coupled_surface + jax.ops.segment_sum(replies, surf_ids, num_segments=NSURF)

    volume_image = volume_field.astype(jnp.float32) + near_part + far_volume + coupled_volume
    surface_image = far_surface + coupled_surface
    return (volume_image, surface_image)
```

```python
import jax
import jax.numpy as jnp
from jax import lax
from jax.experimental import pallas as pl
from jax.experimental.pallas import tpu as pltpu
from jax.sharding import PartitionSpec as P

MESH = pl.DeviceIdType.MESH
F32 = jnp.float32
BF16 = jnp.bfloat16

NX = 4
NZ = 16
NY = 4
NJ = 8
NCELL = NZ * NY
CAP = 4
KINDS = 4
LC = 192
HALF = 96
LS = 128
HW = 48
NN = 27
VX = 256
KH = 128
WIN = 384


def dot(a, b, ca=1, cb=0):
    return lax.dot_general(a, b, (((ca,), (cb,)), ((), ())), preferred_element_type=F32)


def onehot(mask):
    return jnp.where(mask, 1.0, 0.0).astype(BF16)


def iota(shape, dim):
    return lax.broadcasted_iota(jnp.int32, shape, dim)


class Exchange:
    def __init__(self, count, me, device, src, dst, send, recv):
        self.count, self.me, self.device = count, me, device
        self.src, self.dst, self.send, self.recv = src, dst, send, recv

    def copy(self, step, slot):
        target = lax.rem(self.me + step, self.count)
        return pltpu.make_async_remote_copy(
            src_ref=self.src(target),
            dst_ref=self.dst.at[slot],
            send_sem=self.send.at[step],
            recv_sem=self.recv.at[step],
            device_id=self.device(target),
            device_id_type=MESH,
        )

    def loop(self, body):
        def wrapped(step, carry):
            body(step)
            return carry

        lax.fori_loop(1, self.count, wrapped, 0)

    def start(self):
        self.loop(lambda step: self.copy(step, self.me).start())

    def wait_recv(self):
        def body(step):
            source = lax.rem(self.me + self.count - step, self.count)
            self.copy(step, source).wait_recv()

        self.loop(body)

    def wait_send(self):
        self.loop(lambda step: self.copy(step, self.me).wait_send())


def kernel(
    vf, cid, con, near_t, nb_hbm, vrad, srad, vrec, srec, cur, host, lout, lin, tab, sv, pt,
    vout, sout,
    nb, win, halo, msg_info, in_info, mid_info2, all_info,
    msg_cur, in_cur, f_rows, mid_cur, all_cur,
    table, rep_a, rep_b, rep_c, rep_d,
    crow, in_c, mid_c, all_c, up0, xrows, up1, up2, up3,
    lins, tabs, idx_pad, gathered,
    z_send, z_recv, j_send, j_recv, p_send, p_recv, nb_sem,
):
    x = lax.axis_index("sec")
    cell = lax.axis_index("cell")
    c = lax.axis_index("dir")
    z = lax.div(cell, NY)
    y = lax.rem(cell, NY)
    j = y * 2 + c
    g = x * NCELL + cell

    nb_copy = pltpu.make_async_copy(nb_hbm, nb, nb_sem)
    nb_copy.start()

    def z_device(other):
        return (x, other * NY + y, c)

    def j_device(other):
        return (x, z * NY + lax.div(other, 2), lax.rem(other, 2))

    def g_device(step):
        other = lax.rem(g + step + NX * NCELL, NX * NCELL)
        return (lax.div(other, NCELL), lax.rem(other, NCELL), c)

    def x_device(step):
        return (lax.rem(x + step + NX, NX), cell, c)

    barrier = pltpu.get_barrier_semaphore()

    def greet(device):
        pl.semaphore_signal(barrier, inc=1, device_id=device, device_id_type=MESH)

    def greet_z(step, carry):
        greet(z_device(lax.rem(z + step, NZ)))
        return carry

    def greet_j(step, carry):
        greet(j_device(lax.rem(j + step, NJ)))
        return carry

    lax.fori_loop(1, NZ, greet_z, 0)
    lax.fori_loop(1, NJ, greet_j, 0)
    for step in (-1, 1):
        greet(g_device(step))
        greet(x_device(step))

    z_info = Exchange(NZ, z, z_device, lambda t: msg_info.at[t], in_info, z_send.at[0], z_recv.at[0])
    z_cur = Exchange(NZ, z, z_device, lambda t: msg_cur.at[t], in_cur, z_send.at[1], z_recv.at[1])
    z_tree = Exchange(NZ, z, z_device, lambda t: crow, in_c, z_send.at[2], z_recv.at[2])
    z_rep = Exchange(NZ, z, z_device, lambda t: rep_c.at[t], rep_d, z_send.at[3], z_recv.at[3])
    j_info = Exchange(NJ, j, j_device, lambda t: mid_info2, all_info, j_send.at[0], j_recv.at[0])
    j_cur = Exchange(NJ, j, j_device, lambda t: mid_cur.at[t], all_cur, j_send.at[1], j_recv.at[1])
    j_tree = Exchange(NJ, j, j_device, lambda t: mid_c, all_c, j_send.at[2], j_recv.at[2])
    j_rep = Exchange(NJ, j, j_device, lambda t: rep_a.at[t], rep_b, j_send.at[3], j_recv.at[3])

    def pair_copy(number, src, dst, device):
        return pltpu.make_async_remote_copy(
            src_ref=src,
            dst_ref=dst,
            send_sem=p_send.at[number],
            recv_sem=p_recv.at[number],
            device_id=device,
            device_id_type=MESH,
        )

    other_core = (x, cell, 1 - c)
    lin_copy = pair_copy(0, lin, lins.at[c], other_core)
    tab_copy = pair_copy(1, tab, tabs.at[c], other_core)
    halo_right = pair_copy(2, win.at[pl.ds(LC, HW)], halo.at[0], g_device(1))
    halo_left = pair_copy(3, win.at[pl.ds(HW, HW)], halo.at[1], g_device(-1))
    x_right = pair_copy(4, up0.at[:, pl.ds(NCELL, 32)], xrows.at[0], x_device(1))
    x_left = pair_copy(5, up0.at[:, pl.ds(32, 32)], xrows.at[1], x_device(-1))

    with jax.named_scope("pairs_out"):
        rows = [pt[f].astype(F32) for f in range(3)]
        rows = jnp.concatenate(rows + [jnp.zeros((CAP, LS), F32)], axis=0)
        columns = jnp.transpose(rows)
        lane = iota((LS, LS), 1)
        row_low = iota((LS, LS), 0) & (NJ - 1)
        info = jnp.zeros((LS, LS), F32)
        for slot in range(CAP):
            for field in range(2):
                hit = lane == row_low + (field * 32 + slot * NJ)
                info = info + jnp.where(hit, columns[:, 4 + 4 * field + slot][:, None], 0.0)
        spread = onehot((iota((NZ, LS), 1) >> 3) == iota((NZ, LS), 0))
        info = dot(spread, info.astype(BF16))
        for t in range(NZ):
            msg_info[t] = info[t : t + 1]
        own = cur[pl.ds(pl.multiple_of(c * 64, 64), 64), :]
        lane64 = iota((LS, 64), 1).astype(F32)
        parts = []
        for slot in range(CAP):
            pick = onehot(columns[:, slot : slot + 1] == lane64)
            parts.append(dot(pick, own).reshape(NZ, NJ, LS))
        msg_cur[...] = jnp.concatenate(parts, axis=1).astype(BF16)

    pl.semaphore_wait(barrier, (NZ - 1) + (NJ - 1) + 4)
    z_info.start()
    lin_copy.start()
    tab_copy.start()
    z_cur.start()
    in_info[pl.ds(z, 1)] = msg_info[pl.ds(z, 1)]
    in_cur[pl.ds(z, 1)] = msg_cur[pl.ds(z, 1)]
    lins[pl.ds(c, 1)] = lin[...][None]
    tabs[pl.ds(c, 1)] = tab[...][None]

    with jax.named_scope("weighted"):
        ids = cid[...]
        scale = jnp.zeros((LC, VX), F32)
        for m in range(16):
            scale = jnp.where(ids == m, con[m], scale)
        win[pl.ds(HW, LC), :] = (vf[...].astype(F32) * scale).astype(BF16)
    halo_right.start()
    halo_left.start()

    with jax.named_scope("coarse"):
        weighted = win[pl.ds(HW, LC), :]
        outgoing = dot(weighted, vrad[...])
        surf_waves = dot(cur[...], srad[...])
        host_t = onehot(host[...] == iota((LC, LS), 0))
        leaf = lout[...]
        leaf_surf = dot(host_t, leaf, 0, 0)
        coarse = jnp.sum(leaf.astype(F32) * outgoing, axis=0, keepdims=True)
        coarse = coarse + jnp.sum(leaf_surf * surf_waves, axis=0, keepdims=True)
        crow[...] = coarse
    z_tree.start()
    in_c[pl.ds(z, 1)] = crow[...][None]

    with jax.named_scope("reply_table"):
        own_weighted = win[pl.ds(pl.multiple_of(HW + c * HALF, 16), HALF), :]
        for kind in range(KINDS):
            table[pl.ds(kind * HALF, HALF), :] = dot(own_weighted, sv[kind], 1, 1).astype(BF16)

    z_info.wait_recv()
    for t in range(NZ):
        mid_info2[pl.ds(t, 1), :] = in_info[t]
    j_info.start()
    all_info[pl.ds(j, 1)] = mid_info2[...][None]

    z_tree.wait_recv()
    for t in range(NZ):
        mid_c[pl.ds(t, 1), :] = in_c[t]
    j_tree.start()
    all_c[pl.ds(j, 1)] = mid_c[...][None]

    j_info.wait_recv()
    with jax.named_scope("replies"):
        codes = all_info[...].reshape(LS, LS)
        codes = pltpu.roll(codes, lax.rem(LS - j, LS), 1)
        lane384 = iota((LS, KINDS * HALF), 1).astype(F32)
        picks = []
        for slot in range(CAP):
            at = slot * NJ
            code = codes[:, at : at + 1] + HALF * codes[:, 32 + at : 33 + at]
            pick = onehot(code == lane384)
            picks.append(pick)
            rep = dot(pick, table[...]).astype(BF16)
            rep_a[:, slot] = rep.reshape(NJ, NZ, LS)
    j_rep.start()
    rep_b[pl.ds(j, 1)] = rep_a[pl.ds(j, 1)]

    j_tree.wait_recv()
    with jax.named_scope("section_rows"):
        for yy in range(NY):
            for cc in range(2):
                up0[cc, pl.ds(32 + yy, NZ, stride=NY), :] = all_c[2 * yy + cc]
    x_right.start()
    x_left.start()

    z_cur.wait_recv()
    with jax.named_scope("regroup_currents"):
        f_rows[...] = in_cur[...].astype(F32).reshape(NZ * 32, LS)
        for jj in range(NJ):
            for slot in range(CAP):
                block = f_rows[pl.ds(slot * NJ + jj, NZ, stride=32), :]
                mid_cur[jj, slot] = block.astype(BF16)
    j_cur.start()
    all_cur[pl.ds(j, 1)] = mid_cur[pl.ds(j, 1)]

    j_rep.wait_recv()
    with jax.named_scope("regroup_replies"):
        f_rows[...] = rep_b[...].astype(F32).reshape(NJ * 64, LS)
        for zz in range(NZ):
            blocks = [f_rows[pl.ds(slot * NZ + zz, NJ, stride=64), :] for slot in range(CAP)]
            rep_c[zz] = jnp.concatenate(blocks, axis=0).astype(BF16)
    z_rep.start()
    rep_d[pl.ds(z, 1)] = rep_c[pl.ds(z, 1)]

    halo_right.wait_recv()
    halo_left.wait_recv()
    nb_copy.wait()
    with jax.named_scope("near"):
        first = jnp.where(g > 0, 1.0, 0.0)
        last = jnp.where(g < NX * NCELL - 1, 1.0, 0.0)
        win[pl.ds(0, HW), :] = jnp.where(first > 0.5, halo[0].astype(F32), 0.0).astype(BF16)
        win[pl.ds(HW + LC, HW), :] = jnp.where(last > 0.5, halo[1].astype(F32), 0.0).astype(BF16)
        win[pl.ds(2 * HW + LC, WIN - 2 * HW - LC), :] = jnp.zeros((WIN - 2 * HW - LC, VX), BF16)
        idx_pad[...] = jnp.zeros((32, 128), F32)
        idx_pad[pl.ds(0, NN), pl.ds(0, HALF)] = near_t[...].astype(F32)
        slots = jnp.transpose(idx_pad[...])[:HALF]
        lane_w = iota((HALF, WIN), 1).astype(F32)
        window = win[...]
        for n in range(NN):
            pick = onehot(slots[:, n : n + 1] == lane_w)
            gathered[n] = dot(pick, window).astype(BF16)
        near = jnp.zeros((HALF, VX), F32)
        for n in range(NN):
            near = near + dot(gathered[n], nb[n])

    j_cur.wait_recv()
    with jax.named_scope("coupled_volume"):
        sums = jnp.zeros((KINDS * HALF, LS), F32)
        for slot in range(CAP):
            sums = sums + dot(picks[slot], all_cur[:, slot].reshape(LS, LS), 0, 0)
        high = sums.astype(BF16)
        low = (sums - high.astype(F32)).astype(BF16)
        coupled = jnp.zeros((HALF, VX), F32)
        for kind in range(KINDS):
            part = slice(kind * HALF, (kind + 1) * HALF)
            coupled = coupled + dot(high[part], sv[kind]) + dot(low[part], sv[kind])

    x_right.wait_recv()
    x_left.wait_recv()
    tab_copy.wait_recv()
    with jax.named_scope("tree"):
        up0[:, pl.ds(0, 32), :] = jnp.where(x > 0, xrows[0], 0.0)
        up0[:, pl.ds(96, 32), :] = jnp.where(x < NX - 1, xrows[1], 0.0)
        ups = [up0, up1, up2, up3]
        waves = []
        for h in range(2):

            def entry(level, number):
                return tabs[h, level, pl.ds(number, 1), :]

            for level in range(3):
                count = 64 >> level
                even = ups[level][h, pl.ds(0, count, stride=2), :]
                odd = ups[level][h, pl.ds(1, count, stride=2), :]
                ups[level + 1][h] = entry(level, 4) * even + entry(level, 5) * odd
            terms = []
            for level in range(4):
                at = (32 + cell) >> level
                is_odd = (at & 1) == 1

                def row(offset):
                    return ups[level][h, pl.ds(at + offset, 1), :]

                term = jnp.where(is_odd, entry(level, 0) * row(-3), 0.0)
                term = term + entry(level, 1) * row(-2)
                term = term + entry(level, 2) * row(2)
                term = term + jnp.where(is_odd, 0.0, entry(level, 3) * row(3))
                terms.append(term)
            down = terms[3]
            for level in (2, 1, 0):
                is_odd = (((32 + cell) >> level) & 1) == 1
                down = terms[level] + jnp.where(is_odd, entry(level, 7), entry(level, 6)) * down
            waves.append(down)

    lin_copy.wait_recv()
    with jax.named_scope("far"):
        far_volume = jnp.zeros((HALF, VX), F32)
        far_surface = jnp.zeros((64, LS), F32)
        for h in range(2):
            wave = waves[h]
            leaf_own = lins[h, pl.ds(pl.multiple_of(c * HALF, 32), HALF), :].astype(F32)
            incoming = (leaf_own * wave).astype(BF16)
            far_volume = far_volume + dot(incoming, vrec[pl.ds(h * KH, KH), :])
            leaf_all = dot(host_t, lins[h], 0, 0)
            leaf_here = jnp.where(c == 0, leaf_all[:64], leaf_all[64:])
            incoming = (leaf_here * wave).astype(BF16)
            far_surface = far_surface + dot(incoming, srec[pl.ds(h * KH, KH), :])
        field = vf[pl.ds(pl.multiple_of(c * HALF, 32), HALF), :].astype(F32)
        vout[...] = field + near + far_volume + coupled

    z_rep.wait_recv()
    with jax.named_scope("coupled_surface"):
        back = rep_d[...].astype(F32)
        sublane64 = iota((64, LS), 0)
        total = far_surface
        for slot in range(CAP):
            pick = onehot(pt[0, pl.ds(slot, 1), :] == sublane64)
            mine = back[:, slot * NJ : (slot + 1) * NJ, :].reshape(LS, LS).astype(BF16)
            total = total + dot(pick, mine)
        sout[...] = total

    for exchange in (z_info, z_cur, z_tree, z_rep, j_info, j_cur, j_tree, j_rep):
        exchange.wait_send()
    for copy in (lin_copy, tab_copy, halo_right, halo_left, x_right, x_left):
        copy.wait_send()


def on_device(
    volume_field, contrast_id, contrast, near_index, near_blocks, vol_radiation, surf_radiation,
    vol_receive, surf_receive, surface_current, surf_host, leaf_out, leaf_in, level_tables,
    sv_blocks, pair_table,
):
    vmem = pl.BlockSpec(memory_space=pltpu.VMEM)
    specs = [vmem] * 16
    specs[2] = pl.BlockSpec(memory_space=pltpu.SMEM)
    specs[4] = pl.BlockSpec(memory_space=pl.ANY)
    return pl.pallas_call(
        kernel,
        out_shape=(
            jax.ShapeDtypeStruct((HALF, VX), F32),
            jax.ShapeDtypeStruct((64, LS), F32),
        ),
        in_specs=specs,
        out_specs=(vmem, vmem),
        scratch_shapes=[
            pltpu.VMEM((NN, VX, VX), BF16),
            pltpu.VMEM((WIN, VX), BF16),
            pltpu.VMEM((2, HW, VX), BF16),
            pltpu.VMEM((NZ, 1, LS), F32),
            pltpu.VMEM((NZ, 1, LS), F32),
            pltpu.VMEM((NZ, LS), F32),
            pltpu.VMEM((NJ, NZ, LS), F32),
            pltpu.VMEM((NZ, 32, LS), BF16),
            pltpu.VMEM((NZ, 32, LS), BF16),
            pltpu.VMEM((512, LS), F32),
            pltpu.VMEM((NJ, CAP, NZ, LS), BF16),
            pltpu.VMEM((NJ, CAP, NZ, LS), BF16),
            pltpu.VMEM((KINDS * HALF, LS), BF16),
            pltpu.VMEM((NJ, CAP, NZ, LS), BF16),
            pltpu.VMEM((NJ, CAP, NZ, LS), BF16),
            pltpu.VMEM((NZ, 32, LS), BF16),
            pltpu.VMEM((NZ, 32, LS), BF16),
            pltpu.VMEM((1, KH), F32),
            pltpu.VMEM((NZ, 1, KH), F32),
            pltpu.VMEM((NZ, KH), F32),
            pltpu.VMEM((NJ, NZ, KH), F32),
            pltpu.VMEM((2, 128, KH), F32),
            pltpu.VMEM((2, 2, 32, KH), F32),
            pltpu.VMEM((2, 64, KH), F32),
            pltpu.VMEM((2, 32, KH), F32),
            pltpu.VMEM((2, 16, KH), F32),
            pltpu.VMEM((2, LC, KH), BF16),
            pltpu.VMEM((2, 4, 8, KH), F32),
            pltpu.VMEM((32, 128), F32),
            pltpu.VMEM((NN, HALF, VX), BF16),
            pltpu.SemaphoreType.DMA((4, NZ)),
            pltpu.SemaphoreType.DMA((4, NZ)),
            pltpu.SemaphoreType.DMA((4, NJ)),
            pltpu.SemaphoreType.DMA((4, NJ)),
            pltpu.SemaphoreType.DMA((6,)),
            pltpu.SemaphoreType.DMA((6,)),
            pltpu.SemaphoreType.DMA,
        ],
        compiler_params=pltpu.CompilerParams(
            collective_id=0, has_side_effects=True, vmem_limit_bytes=40 * 1024 * 1024
        ),
    )(
        volume_field, contrast_id, contrast, near_index.T, near_blocks, vol_radiation,
        surf_radiation, vol_receive, surf_receive, surface_current, surf_host.reshape(1, LS),
        leaf_out, leaf_in, level_tables, sv_blocks, jnp.transpose(pair_table, (2, 1, 0)),
    )


def solution(mesh):
    in_specs = (
        P(("sec", "cell"), None),
        P(("sec", "cell"), None),
        P(),
        P(("sec", "cell", "dir"), None),
        P(),
        P(None, "dir"),
        P(None, "dir"),
        P(),
        P(),
        P(("sec", "cell"), None),
        P(("sec", "cell")),
        P(None, "dir"),
        P(None, "dir"),
        P(None, None, "dir"),
        P(),
        P(("sec", "cell", "dir"), None, None),
    )
    out_specs = (P(("sec", "cell", "dir"), None), P(("sec", "cell", "dir"), None))
    return jax.shard_map(
        on_device, mesh=mesh, in_specs=in_specs, out_specs=out_specs, check_vma=False
    )
```

```python
import jax
import jax.numpy as jnp
from jax import lax
from jax.experimental import pallas as pl
from jax.experimental.pallas import tpu as pltpu
from jax.sharding import PartitionSpec as P

MESH = pl.DeviceIdType.MESH
F32 = jnp.float32
BF16 = jnp.bfloat16

NX = 4
NZ = 16
NY = 4
NJ = 8
NCELL = NZ * NY
CAP = 4
KINDS = 4
LC = 192
HALF = 96
LS = 128
HW = 48
NN = 27
VX = 256
KH = 128
WIN = 384


def dot(a, b, ca=1, cb=0):
    return lax.dot_general(a, b, (((ca,), (cb,)), ((), ())), preferred_element_type=F32)


def onehot(mask):
    return jnp.where(mask, 1.0, 0.0).astype(BF16)


def iota(shape, dim):
    return lax.broadcasted_iota(jnp.int32, shape, dim)


class Exchange:
    def __init__(self, count, me, device, src, dst, send, recv):
        self.count, self.me, self.device = count, me, device
        self.src, self.dst, self.send, self.recv = src, dst, send, recv

    def copy(self, step, slot):
        target = lax.rem(self.me + self.offset(step), self.count)
        return pltpu.make_async_remote_copy(
            src_ref=self.src(target),
            dst_ref=self.dst.at[slot],
            send_sem=self.send.at[step],
            recv_sem=self.recv.at[step],
            device_id=self.device(target),
            device_id_type=MESH,
        )

    def offset(self, step):
        low = lax.div(self.count + 1 - step, 2)
        return jnp.where(lax.rem(step, 2) == 1, low, self.count - low)

    def loop(self, body):
        def wrapped(step, carry):
            body(step)
            return carry

        lax.fori_loop(1, self.count, wrapped, 0)

    def start(self):
        self.loop(lambda step: self.copy(step, self.me).start())

    def wait_recv(self):
        def body(step):
            source = lax.rem(self.me + self.count - self.offset(step), self.count)
            self.copy(step, source).wait_recv()

        self.loop(body)

    def wait_send(self):
        self.loop(lambda step: self.copy(step, self.me).wait_send())


def kernel(
    vf_in, cid_in, con_in, near_in, nb_in, vrad_in, srad_in, vrec_in, srec_in, cur_in, host_in,
    lout_in, lin_in, tab_in, sv_in, pt_in,
    vout, sout,
    vf, cid, con, near_t, nb, vrad, srad, vrec, srec, cur, host, lout, sv, pt, win, halo, msg, in_info, mid_info, all_info, crow, in_c, mid_c, all_c,
    msg_cur, in_cur, f_rows, mid_cur, all_cur,
    table, rep_a, rep_b, rep_c, rep_d,
    up0, xrows, up1, up2, up3,
    lins, tabs, idx_pad, gathered,
    z_send, z_recv, j_send, j_recv, p_send, p_recv, load_sem,
):
    x = lax.axis_index("sec")
    cell = lax.axis_index("cell")
    c = lax.axis_index("dir")
    z = lax.div(cell, NY)
    y = lax.rem(cell, NY)
    j = y * 2 + c
    g = x * NCELL + cell

    loads = {}
    order = [
        ("pt", pt_in, pt), ("cur", cur_in, cur), ("cid", cid_in, cid), ("vf", vf_in, vf),
        ("con", con_in, con), ("vrad", vrad_in, vrad), ("srad", srad_in, srad),
        ("host", host_in, host), ("lout", lout_in, lout), ("sv", sv_in, sv),
        ("near", near_in, near_t), ("lin", lin_in, lins.at[c]), ("tab", tab_in, tabs.at[c]),
        ("nb", nb_in, nb), ("vrec", vrec_in, vrec), ("srec", srec_in, srec),
    ]
    for number, (name, src, dst) in enumerate(order):
        loads[name] = pltpu.make_async_copy(src, dst, load_sem.at[number])
    loads["pt"].start()

    def loaded(*names):
        for name in names:
            loads[name].wait()

    def z_device(other):
        return (x, other * NY + y, c)

    def j_device(other):
        return (x, z * NY + lax.div(other, 2), lax.rem(other, 2))

    def g_device(step):
        other = lax.rem(g + step + NX * NCELL, NX * NCELL)
        return (lax.div(other, NCELL), lax.rem(other, NCELL), c)

    def x_device(step):
        return (lax.rem(x + step + NX, NX), cell, c)

    barrier = pltpu.get_barrier_semaphore()

    def greet(device):
        pl.semaphore_signal(barrier, inc=1, device_id=device, device_id_type=MESH)

    def greet_z(step, carry):
        greet(z_device(lax.rem(z + step, NZ)))
        return carry

    def greet_j(step, carry):
        greet(j_device(lax.rem(j + step, NJ)))
        return carry

    lax.fori_loop(1, NZ, greet_z, 0)
    lax.fori_loop(1, NJ, greet_j, 0)
    for step in (-1, 1):
        greet(g_device(step))
        greet(x_device(step))
    for name in loads:
        if name != "pt":
            loads[name].start()

    z_info = Exchange(NZ, z, z_device, lambda t: msg.at[t], in_info, z_send.at[0], z_recv.at[0])
    z_cur = Exchange(NZ, z, z_device, lambda t: msg_cur.at[t], in_cur, z_send.at[1], z_recv.at[1])
    z_rep = Exchange(NZ, z, z_device, lambda t: rep_c.at[t], rep_d, z_send.at[2], z_recv.at[2])
    z_tree = Exchange(NZ, z, z_device, lambda t: crow, in_c, z_send.at[3], z_recv.at[3])
    j_info = Exchange(NJ, j, j_device, lambda t: mid_info, all_info, j_send.at[0], j_recv.at[0])
    j_cur = Exchange(NJ, j, j_device, lambda t: mid_cur.at[t], all_cur, j_send.at[1], j_recv.at[1])
    j_rep = Exchange(NJ, j, j_device, lambda t: rep_a.at[t], rep_b, j_send.at[2], j_recv.at[2])
    j_tree = Exchange(NJ, j, j_device, lambda t: mid_c, all_c, j_send.at[3], j_recv.at[3])

    def pair_copy(number, src, dst, device):
        return pltpu.make_async_remote_copy(
            src_ref=src,
            dst_ref=dst,
            send_sem=p_send.at[number],
            recv_sem=p_recv.at[number],
            device_id=device,
            device_id_type=MESH,
        )

    other_core = (x, cell, 1 - c)
    lin_copy = pair_copy(0, lin_in, lins.at[c], other_core)
    tab_copy = pair_copy(1, tab_in, tabs.at[c], other_core)
    halo_right = pair_copy(2, win.at[pl.ds(LC, HW)], halo.at[0], g_device(1))
    halo_left = pair_copy(3, win.at[pl.ds(HW, HW)], halo.at[1], g_device(-1))
    x_right = pair_copy(4, up0.at[:, pl.ds(NCELL, 32)], xrows.at[0], x_device(1))
    x_left = pair_copy(5, up0.at[:, pl.ds(32, 32)], xrows.at[1], x_device(-1))

    loaded("pt")
    with jax.named_scope("pairs_out"):
        rows = [pt[f].astype(F32) for f in range(3)]
        rows = jnp.concatenate(rows + [jnp.zeros((CAP, LS), F32)], axis=0)
        columns = jnp.transpose(rows)
        lane = iota((LS, LS), 1)
        row_low = iota((LS, LS), 0) & (NJ - 1)
        info = jnp.zeros((LS, LS), F32)
        for slot in range(CAP):
            for field in range(2):
                hit = lane == row_low + (field * 32 + slot * NJ)
                info = info + jnp.where(hit, columns[:, 4 + 4 * field + slot][:, None], 0.0)
        spread = onehot((iota((NZ, LS), 1) >> 3) == iota((NZ, LS), 0))
        info = dot(spread, info.astype(BF16))
        for t in range(NZ):
            msg[t] = info[t : t + 1]
    with jax.named_scope("barrier"):
        pl.semaphore_wait(barrier, (NZ - 1) + (NJ - 1) + 4)
    with jax.named_scope("start_z_info"):
        z_info.start()
    in_info[pl.ds(z, 1)] = msg[pl.ds(z, 1)]

    loaded("cid", "vf", "con")
    with jax.named_scope("weighted"):
        ids = cid[...]
        scale = jnp.zeros((LC, VX), F32)
        for m in range(16):
            scale = jnp.where(ids == m, con[m], scale)
        win[pl.ds(HW, LC), :] = (vf[...].astype(F32) * scale).astype(BF16)
    loaded("vrad", "cur", "srad", "host", "lout")
    with jax.named_scope("coarse"):
        weighted = win[pl.ds(HW, LC), :]
        outgoing = dot(weighted, vrad[...])
        surf_waves = dot(cur[...], srad[...])
        host_t = onehot(host[...] == iota((LC, LS), 0))
        leaf = lout[...]
        leaf_surf = dot(host_t, leaf, 0, 0)
        coarse = jnp.sum(leaf.astype(F32) * outgoing, axis=0, keepdims=True)
        coarse = coarse + jnp.sum(leaf_surf * surf_waves, axis=0, keepdims=True)
        crow[...] = coarse
    with jax.named_scope("start_z_tree"):
        z_tree.start()
        halo_right.start()
        halo_left.start()
        lin_copy.start()
        tab_copy.start()
    in_c[pl.ds(z, 1)] = crow[...][None]

    with jax.named_scope("currents_out"):
        own = cur[pl.ds(pl.multiple_of(c * 64, 64), 64), :]
        lane64 = iota((LS, 64), 1).astype(F32)
        parts = []
        for slot in range(CAP):
            pick = onehot(columns[:, slot : slot + 1] == lane64)
            parts.append(dot(pick, own).reshape(NZ, NJ, LS))
        msg_cur[...] = jnp.concatenate(parts, axis=1).astype(BF16)

    in_cur[pl.ds(z, 1)] = msg_cur[pl.ds(z, 1)]

    loaded("sv")
    with jax.named_scope("reply_table"):
        own_weighted = win[pl.ds(pl.multiple_of(HW + c * HALF, 16), HALF), :]
        for kind in range(KINDS):
            table[pl.ds(kind * HALF, HALF), :] = dot(own_weighted, sv[kind], 1, 1).astype(BF16)

    with jax.named_scope("wait_z_info"):
        z_info.wait_recv()
    for t in range(NZ):
        mid_info[pl.ds(t, 1), :] = in_info[t]
    with jax.named_scope("start_j_info"):
        j_info.start()
    all_info[pl.ds(j, 1)] = mid_info[...][None]
    with jax.named_scope("wait_z_tree"):
        z_tree.wait_recv()
    for t in range(NZ):
        mid_c[pl.ds(t, 1), :] = in_c[t]
    j_tree.start()
    with jax.named_scope("start_z_cur"):
        z_cur.start()
    all_c[pl.ds(j, 1)] = mid_c[...][None]
    with jax.named_scope("wait_j_info"):
        j_info.wait_recv()
    with jax.named_scope("replies"):
        codes = all_info[...].reshape(LS, LS)
        codes = pltpu.roll(codes, lax.rem(LS - j, LS), 1)
        lane384 = iota((LS, KINDS * HALF), 1).astype(F32)
        picks = []
        for slot in range(CAP):
            at = slot * NJ
            code = codes[:, at : at + 1] + HALF * codes[:, 32 + at : 33 + at]
            pick = onehot(code == lane384)
            picks.append(pick)
            rep = dot(pick, table[...]).astype(BF16)
            rep_a[:, slot] = rep.reshape(NJ, NZ, LS)
    j_rep.start()
    rep_b[pl.ds(j, 1)] = rep_a[pl.ds(j, 1)]
    with jax.named_scope("wait_halo"):
        halo_right.wait_recv()
        halo_left.wait_recv()
        loaded("near", "nb")
    with jax.named_scope("near"):
        first = jnp.where(g > 0, 1.0, 0.0)
        last = jnp.where(g < NX * NCELL - 1, 1.0, 0.0)
        win[pl.ds(0, HW), :] = jnp.where(first > 0.5, halo[0].astype(F32), 0.0).astype(BF16)
        win[pl.ds(HW + LC, HW), :] = jnp.where(last > 0.5, halo[1].astype(F32), 0.0).astype(BF16)
        win[pl.ds(2 * HW + LC, WIN - 2 * HW - LC), :] = jnp.zeros((WIN - 2 * HW - LC, VX), BF16)
        idx_pad[...] = jnp.zeros((32, 128), F32)
        idx_pad[pl.ds(0, NN), pl.ds(0, HALF)] = near_t[...].astype(F32)
        slots = jnp.transpose(idx_pad[...])[:HALF]
        lane_w = iota((HALF, WIN), 1).astype(F32)
        window = win[...]
        for n in range(NN):
            pick = onehot(slots[:, n : n + 1] == lane_w)
            gathered[n] = dot(pick, window).astype(BF16)
        near = jnp.zeros((HALF, VX), F32)
        for n in range(NN):
            near = near + dot(gathered[n], nb[n])

    with jax.named_scope("wait_j_tree"):
        j_tree.wait_recv()
    with jax.named_scope("section_rows"):
        for yy in range(NY):
            for cc in range(2):
                up0[cc, pl.ds(32 + yy, NZ, stride=NY), :] = all_c[2 * yy + cc]
    x_right.start()
    x_left.start()

    with jax.named_scope("wait_j_rep"):
        j_rep.wait_recv()
    with jax.named_scope("regroup_replies"):
        f_rows[...] = rep_b[...].astype(F32).reshape(NJ * 64, LS)
        for zz in range(NZ):
            blocks = [f_rows[pl.ds(slot * NZ + zz, NJ, stride=64), :] for slot in range(CAP)]
            rep_c[zz] = jnp.concatenate(blocks, axis=0).astype(BF16)
    with jax.named_scope("start_z_rep"):
        z_rep.start()
    rep_d[pl.ds(z, 1)] = rep_c[pl.ds(z, 1)]

    with jax.named_scope("wait_z_cur"):
        z_cur.wait_recv()
    with jax.named_scope("regroup_currents"):
        f_rows[...] = in_cur[...].astype(F32).reshape(NZ * 32, LS)
        for jj in range(NJ):
            for slot in range(CAP):
                block = f_rows[pl.ds(slot * NJ + jj, NZ, stride=32), :]
                mid_cur[jj, slot] = block.astype(BF16)
    j_cur.start()
    all_cur[pl.ds(j, 1)] = mid_cur[pl.ds(j, 1)]

    with jax.named_scope("wait_x"):
        x_right.wait_recv()
        x_left.wait_recv()
    loaded("tab")
    tab_copy.wait_recv()
    with jax.named_scope("tree"):
        up0[:, pl.ds(0, 32), :] = jnp.where(x > 0, xrows[0], 0.0)
        up0[:, pl.ds(96, 32), :] = jnp.where(x < NX - 1, xrows[1], 0.0)
        ups = [up0, up1, up2, up3]
        waves = []
        for h in range(2):

            def entry(level, number):
                return tabs[h, level, pl.ds(number, 1), :]

            for level in range(3):
                count = 64 >> level
                even = ups[level][h, pl.ds(0, count, stride=2), :]
                odd = ups[level][h, pl.ds(1, count, stride=2), :]
                ups[level + 1][h] = entry(level, 4) * even + entry(level, 5) * odd
            terms = []
            for level in range(4):
                at = (32 + cell) >> level
                is_odd = (at & 1) == 1

                def row(offset):
                    return ups[level][h, pl.ds(at + offset, 1), :]

                term = jnp.where(is_odd, entry(level, 0) * row(-3), 0.0)
                term = term + entry(level, 1) * row(-2)
                term = term + entry(level, 2) * row(2)
                term = term + jnp.where(is_odd, 0.0, entry(level, 3) * row(3))
                terms.append(term)
            down = terms[3]
            for level in (2, 1, 0):
                is_odd = (((32 + cell) >> level) & 1) == 1
                down = terms[level] + jnp.where(is_odd, entry(level, 7), entry(level, 6)) * down
            waves.append(down)

    loaded("lin", "vrec", "srec")
    lin_copy.wait_recv()
    with jax.named_scope("far"):
        far_volume = jnp.zeros((HALF, VX), F32)
        far_surface = jnp.zeros((64, LS), F32)
        for h in range(2):
            wave = waves[h]
            leaf_own = lins[h, pl.ds(pl.multiple_of(c * HALF, 32), HALF), :].astype(F32)
            incoming = (leaf_own * wave).astype(BF16)
            far_volume = far_volume + dot(incoming, vrec[pl.ds(h * KH, KH), :])
            leaf_all = dot(host_t, lins[h], 0, 0)
            leaf_here = jnp.where(c == 0, leaf_all[:64], leaf_all[64:])
            incoming = (leaf_here * wave).astype(BF16)
            far_surface = far_surface + dot(incoming, srec[pl.ds(h * KH, KH), :])
    with jax.named_scope("wait_j_cur"):
        j_cur.wait_recv()
    with jax.named_scope("coupled_volume"):
        sums = jnp.zeros((KINDS * HALF, LS), F32)
        for slot in range(CAP):
            sums = sums + dot(picks[slot], all_cur[:, slot].reshape(LS, LS), 0, 0)
        high = sums.astype(BF16)
        low = (sums - high.astype(F32)).astype(BF16)
        coupled = jnp.zeros((HALF, VX), F32)
        for kind in range(KINDS):
            part = slice(kind * HALF, (kind + 1) * HALF)
            coupled = coupled + dot(high[part], sv[kind]) + dot(low[part], sv[kind])

    with jax.named_scope("volume_out"):
        field = vf[pl.ds(pl.multiple_of(c * HALF, 32), HALF), :].astype(F32)
        vout[...] = field + near + far_volume + coupled

    with jax.named_scope("wait_sends"):
        for exchange in (z_info, z_cur, z_tree, j_info, j_cur, j_rep, j_tree):
            exchange.wait_send()
        for copy in (lin_copy, tab_copy, halo_right, halo_left, x_right, x_left):
            copy.wait_send()
    with jax.named_scope("wait_z_rep"):
        z_rep.wait_recv()
    with jax.named_scope("coupled_surface"):
        back = rep_d[...].astype(F32)
        sublane64 = iota((64, LS), 0)
        total = far_surface
        for slot in range(CAP):
            pick = onehot(pt[0, pl.ds(slot, 1), :] == sublane64)
            mine = back[:, slot * NJ : (slot + 1) * NJ, :].reshape(LS, LS).astype(BF16)
            total = total + dot(pick, mine)
        sout[...] = total

    z_rep.wait_send()


def on_device(
    volume_field, contrast_id, contrast, near_index, near_blocks, vol_radiation, surf_radiation,
    vol_receive, surf_receive, surface_current, surf_host, leaf_out, leaf_in, level_tables,
    sv_blocks, pair_table,
):
    inputs = (
        volume_field, contrast_id, contrast, near_index.T, near_blocks, vol_radiation,
        surf_radiation, vol_receive, surf_receive, surface_current, surf_host.reshape(1, LS),
        leaf_out, leaf_in, level_tables, sv_blocks, jnp.transpose(pair_table, (2, 1, 0)),
    )
    hbm = pl.BlockSpec(memory_space=pltpu.HBM)
    vmem = pl.BlockSpec(memory_space=pltpu.VMEM)
    specs = [hbm] * 16
    shapes = (jax.ShapeDtypeStruct((HALF, VX), F32), jax.ShapeDtypeStruct((64, LS), F32))
    return pl.pallas_call(
        kernel,
        out_shape=shapes,
        in_specs=specs,
        out_specs=(vmem, vmem),
        scratch_shapes=[
            pltpu.VMEM((LC, VX), BF16),
            pltpu.VMEM((LC, VX), jnp.int32),
            pltpu.SMEM((16,), F32),
            pltpu.VMEM((NN, HALF), jnp.int32),
            pltpu.VMEM((NN, VX, VX), BF16),
            pltpu.VMEM((VX, KH), BF16),
            pltpu.VMEM((LS, KH), BF16),
            pltpu.VMEM((2 * KH, VX), BF16),
            pltpu.VMEM((2 * KH, LS), BF16),
            pltpu.VMEM((LS, LS), BF16),
            pltpu.VMEM((1, LS), jnp.int32),
            pltpu.VMEM((LC, KH), BF16),
            pltpu.VMEM((KINDS, LS, VX), BF16),
            pltpu.VMEM((3, CAP, LS), jnp.int32),
            pltpu.VMEM((WIN, VX), BF16),
            pltpu.VMEM((2, HW, VX), BF16),
            pltpu.VMEM((NZ, 1, LS), F32),
            pltpu.VMEM((NZ, 1, LS), F32),
            pltpu.VMEM((NZ, LS), F32),
            pltpu.VMEM((NJ, NZ, LS), F32),
            pltpu.VMEM((1, KH), F32),
            pltpu.VMEM((NZ, 1, KH), F32),
            pltpu.VMEM((NZ, KH), F32),
            pltpu.VMEM((NJ, NZ, KH), F32),
            pltpu.VMEM((NZ, 32, LS), BF16),
            pltpu.VMEM((NZ, 32, LS), BF16),
            pltpu.VMEM((512, LS), F32),
            pltpu.VMEM((NJ, CAP, NZ, LS), BF16),
            pltpu.VMEM((NJ, CAP, NZ, LS), BF16),
            pltpu.VMEM((KINDS * HALF, LS), BF16),
            pltpu.VMEM((NJ, CAP, NZ, LS), BF16),
            pltpu.VMEM((NJ, CAP, NZ, LS), BF16),
            pltpu.VMEM((NZ, 32, LS), BF16),
            pltpu.VMEM((NZ, 32, LS), BF16),
            pltpu.VMEM((2, 128, KH), F32),
            pltpu.VMEM((2, 2, 32, KH), F32),
            pltpu.VMEM((2, 64, KH), F32),
            pltpu.VMEM((2, 32, KH), F32),
            pltpu.VMEM((2, 16, KH), F32),
            pltpu.VMEM((2, LC, KH), BF16),
            pltpu.VMEM((2, 4, 8, KH), F32),
            pltpu.VMEM((32, 128), F32),
            pltpu.VMEM((NN, HALF, VX), BF16),
            pltpu.SemaphoreType.DMA((4, NZ)),
            pltpu.SemaphoreType.DMA((4, NZ)),
            pltpu.SemaphoreType.DMA((4, NJ)),
            pltpu.SemaphoreType.DMA((4, NJ)),
            pltpu.SemaphoreType.DMA((6,)),
            pltpu.SemaphoreType.DMA((6,)),
            pltpu.SemaphoreType.DMA((16,)),
        ],
        compiler_params=pltpu.CompilerParams(
            collective_id=0, has_side_effects=True, vmem_limit_bytes=40 * 1024 * 1024
        ),
    )(*[pltpu.with_memory_space_constraint(array, pltpu.HBM) for array in inputs])


def solution(mesh):
    in_specs = (
        P(("sec", "cell"), None),
        P(("sec", "cell"), None),
        P(),
        P(("sec", "cell", "dir"), None),
        P(),
        P(None, "dir"),
        P(None, "dir"),
        P(),
        P(),
        P(("sec", "cell"), None),
        P(("sec", "cell")),
        P(None, "dir"),
        P(None, "dir"),
        P(None, None, "dir"),
        P(),
        P(("sec", "cell", "dir"), None, None),
    )
    out_specs = (P(("sec", "cell", "dir"), None), P(("sec", "cell", "dir"), None))
    return jax.shard_map(
        on_device, mesh=mesh, in_specs=in_specs, out_specs=out_specs, check_vma=False
    )
```

```python
import jax
import jax.numpy as jnp
from jax import lax
from jax.experimental import pallas as pl
from jax.experimental.pallas import tpu as pltpu
from jax.sharding import PartitionSpec as P

MESH = pl.DeviceIdType.MESH
F32 = jnp.float32
BF16 = jnp.bfloat16

NX = 4
NZ = 16
NY = 4
NJ = 8
NCELL = NZ * NY
CAP = 4
KINDS = 4
LC = 192
HALF = 96
LS = 128
HW = 48
NN = 27
VX = 256
KH = 128
WIN = 384


def dot(a, b, ca=1, cb=0):
    return lax.dot_general(a, b, (((ca,), (cb,)), ((), ())), preferred_element_type=F32)


def onehot(mask):
    return jnp.where(mask, 1.0, 0.0).astype(BF16)


def iota(shape, dim):
    return lax.broadcasted_iota(jnp.int32, shape, dim)


class Exchange:
    def __init__(self, count, me, device, src, dst, send, recv):
        self.count, self.me, self.device = count, me, device
        self.src, self.dst, self.send, self.recv = src, dst, send, recv

    def start(self):
        def body(step, carry):
            low = lax.div(self.count + 1 - step, 2)
            offset = jnp.where(lax.rem(step, 2) == 1, low, self.count - low)
            target = lax.rem(self.me + offset, self.count)
            pltpu.make_async_remote_copy(
                src_ref=self.src(target),
                dst_ref=self.dst.at[self.me],
                send_sem=self.send,
                recv_sem=self.recv,
                device_id=self.device(target),
                device_id_type=MESH,
            ).start()
            return carry

        lax.fori_loop(1, self.count, body, 0)

    def all_blocks(self):
        blocks = self.dst.at[pl.ds(0, self.count - 1)]
        return pltpu.make_async_remote_copy(
            src_ref=blocks,
            dst_ref=blocks,
            send_sem=self.send,
            recv_sem=self.recv,
            device_id=self.device(lax.rem(self.me + 1, self.count)),
            device_id_type=MESH,
        )

    def wait_recv(self):
        self.all_blocks().wait_recv()

    def wait_send(self):
        self.all_blocks().wait_send()


def kernel(
    vf_in, cid_in, con_in, near_in, nb_in, vrad_in, srad_in, vrec_in, srec_in, cur_in, host_in,
    lout_in, lin_in, tab_in, sv_in, pt_in,
    vout, sout,
    vf, cid, con, near_t, nb, vrad, srad, vrec, srec, cur, host, lout, sv, pt, win, halo, msg, in_info, mid_info, all_info, crow, in_c, mid_c, all_c,
    msg_cur, in_cur, f_rows, mid_cur, all_cur,
    table, rep_a, rep_b, rep_c, rep_d,
    up0, xrows, up1, up2, up3,
    lins, tabs, idx_pad, gathered,
    z_send, z_recv, j_send, j_recv, p_send, p_recv, load_sem,
):
    x = lax.axis_index("sec")
    cell = lax.axis_index("cell")
    c = lax.axis_index("dir")
    z = lax.div(cell, NY)
    y = lax.rem(cell, NY)
    j = y * 2 + c
    g = x * NCELL + cell

    loads = {}
    order = [
        ("pt", pt_in, pt), ("cur", cur_in, cur), ("cid", cid_in, cid), ("vf", vf_in, vf),
        ("con", con_in, con), ("vrad", vrad_in, vrad), ("srad", srad_in, srad),
        ("host", host_in, host), ("lout", lout_in, lout), ("sv", sv_in, sv),
        ("near", near_in, near_t), ("lin", lin_in, lins.at[c]), ("tab", tab_in, tabs.at[c]),
        ("nb", nb_in, nb), ("vrec", vrec_in, vrec), ("srec", srec_in, srec),
    ]
    for number, (name, src, dst) in enumerate(order):
        loads[name] = pltpu.make_async_copy(src, dst, load_sem.at[number])
    loads["pt"].start()

    def loaded(*names):
        for name in names:
            loads[name].wait()

    def z_device(other):
        return (x, other * NY + y, c)

    def j_device(other):
        return (x, z * NY + lax.div(other, 2), lax.rem(other, 2))

    def g_device(step):
        other = lax.rem(g + step + NX * NCELL, NX * NCELL)
        return (lax.div(other, NCELL), lax.rem(other, NCELL), c)

    def x_device(step):
        return (lax.rem(x + step + NX, NX), cell, c)

    barrier = pltpu.get_barrier_semaphore()

    def greet(device):
        pl.semaphore_signal(barrier, inc=1, device_id=device, device_id_type=MESH)

    def greet_z(step, carry):
        greet(z_device(lax.rem(z + step, NZ)))
        return carry

    def greet_j(step, carry):
        greet(j_device(lax.rem(j + step, NJ)))
        return carry

    lax.fori_loop(1, NZ, greet_z, 0)
    lax.fori_loop(1, NJ, greet_j, 0)
    for step in (-1, 1):
        greet(g_device(step))
        greet(x_device(step))
    for name in loads:
        if name != "pt":
            loads[name].start()

    z_info = Exchange(NZ, z, z_device, lambda t: msg.at[t], in_info, z_send.at[0], z_recv.at[0])
    z_cur = Exchange(NZ, z, z_device, lambda t: msg_cur.at[t], in_cur, z_send.at[1], z_recv.at[1])
    z_rep = Exchange(NZ, z, z_device, lambda t: rep_c.at[t], rep_d, z_send.at[2], z_recv.at[2])
    z_tree = Exchange(NZ, z, z_device, lambda t: crow, in_c, z_send.at[3], z_recv.at[3])
    j_info = Exchange(NJ, j, j_device, lambda t: mid_info, all_info, j_send.at[0], j_recv.at[0])
    j_cur = Exchange(NJ, j, j_device, lambda t: mid_cur.at[t], all_cur, j_send.at[1], j_recv.at[1])
    j_rep = Exchange(NJ, j, j_device, lambda t: rep_a.at[t], rep_b, j_send.at[2], j_recv.at[2])
    j_tree = Exchange(NJ, j, j_device, lambda t: mid_c, all_c, j_send.at[3], j_recv.at[3])

    def pair_copy(number, src, dst, device):
        return pltpu.make_async_remote_copy(
            src_ref=src,
            dst_ref=dst,
            send_sem=p_send.at[number],
            recv_sem=p_recv.at[number],
            device_id=device,
            device_id_type=MESH,
        )

    other_core = (x, cell, 1 - c)
    lin_copy = pair_copy(0, lin_in, lins.at[c], other_core)
    tab_copy = pair_copy(1, tab_in, tabs.at[c], other_core)
    halo_right = pair_copy(2, win.at[pl.ds(LC, HW)], halo.at[0], g_device(1))
    halo_left = pair_copy(3, win.at[pl.ds(HW, HW)], halo.at[1], g_device(-1))
    x_right = pair_copy(4, up0.at[:, pl.ds(NCELL, 32)], xrows.at[0], x_device(1))
    x_left = pair_copy(5, up0.at[:, pl.ds(32, 32)], xrows.at[1], x_device(-1))

    loaded("pt")
    with jax.named_scope("pairs_out"):
        rows = [pt[f].astype(F32) for f in range(3)]
        rows = jnp.concatenate(rows + [jnp.zeros((CAP, LS), F32)], axis=0)
        columns = jnp.transpose(rows)
        lane = iota((LS, LS), 1)
        row_low = iota((LS, LS), 0) & (NJ - 1)
        info = jnp.zeros((LS, LS), F32)
        for slot in range(CAP):
            for field in range(2):
                hit = lane == row_low + (field * 32 + slot * NJ)
                info = info + jnp.where(hit, columns[:, 4 + 4 * field + slot][:, None], 0.0)
        spread = onehot((iota((NZ, LS), 1) >> 3) == iota((NZ, LS), 0))
        info = dot(spread, info.astype(BF16))
        for t in range(NZ):
            msg[t] = info[t : t + 1]
    with jax.named_scope("barrier"):
        pl.semaphore_wait(barrier, (NZ - 1) + (NJ - 1) + 4)
    with jax.named_scope("start_z_info"):
        z_info.start()
    in_info[pl.ds(z, 1)] = msg[pl.ds(z, 1)]

    loaded("cid", "vf", "con")
    with jax.named_scope("weighted"):
        ids = cid[...]
        scale = jnp.zeros((LC, VX), F32)
        for m in range(16):
            scale = jnp.where(ids == m, con[m], scale)
        win[pl.ds(HW, LC), :] = (vf[...].astype(F32) * scale).astype(BF16)
    loaded("vrad", "cur", "srad", "host", "lout")
    with jax.named_scope("coarse"):
        weighted = win[pl.ds(HW, LC), :]
        outgoing = dot(weighted, vrad[...])
        surf_waves = dot(cur[...], srad[...])
        host_t = onehot(host[...] == iota((LC, LS), 0))
        leaf = lout[...]
        leaf_surf = dot(host_t, leaf, 0, 0)
        coarse = jnp.sum(leaf.astype(F32) * outgoing, axis=0, keepdims=True)
        coarse = coarse + jnp.sum(leaf_surf * surf_waves, axis=0, keepdims=True)
        crow[...] = coarse
    with jax.named_scope("start_z_tree"):
        z_tree.start()
        halo_right.start()
        halo_left.start()
        lin_copy.start()
        tab_copy.start()
    in_c[pl.ds(z, 1)] = crow[...][None]

    with jax.named_scope("currents_out"):
        own = cur[pl.ds(pl.multiple_of(c * 64, 64), 64), :]
        lane64 = iota((LS, 64), 1).astype(F32)
        parts = []
        for slot in range(CAP):
            pick = onehot(columns[:, slot : slot + 1] == lane64)
            parts.append(dot(pick, own).reshape(NZ, NJ, LS))
        msg_cur[...] = jnp.concatenate(parts, axis=1).astype(BF16)

    in_cur[pl.ds(z, 1)] = msg_cur[pl.ds(z, 1)]

    loaded("sv")
    with jax.named_scope("reply_table"):
        own_weighted = win[pl.ds(pl.multiple_of(HW + c * HALF, 16), HALF), :]
        for kind in range(KINDS):
            table[pl.ds(kind * HALF, HALF), :] = dot(own_weighted, sv[kind], 1, 1).astype(BF16)

    with jax.named_scope("wait_z_info"):
        z_info.wait_recv()
    for t in range(NZ):
        mid_info[pl.ds(t, 1), :] = in_info[t]
    with jax.named_scope("start_j_info"):
        j_info.start()
    all_info[pl.ds(j, 1)] = mid_info[...][None]
    with jax.named_scope("wait_z_tree"):
        z_tree.wait_recv()
    for t in range(NZ):
        mid_c[pl.ds(t, 1), :] = in_c[t]
    j_tree.start()
    with jax.named_scope("start_z_cur"):
        z_cur.start()
    all_c[pl.ds(j, 1)] = mid_c[...][None]
    with jax.named_scope("wait_j_info"):
        j_info.wait_recv()
    with jax.named_scope("replies"):
        codes = all_info[...].reshape(LS, LS)
        codes = pltpu.roll(codes, lax.rem(LS - j, LS), 1)
        lane384 = iota((LS, KINDS * HALF), 1).astype(F32)
        picks = []
        for slot in range(CAP):
            at = slot * NJ
            code = codes[:, at : at + 1] + HALF * codes[:, 32 + at : 33 + at]
            pick = onehot(code == lane384)
            picks.append(pick)
            rep = dot(pick, table[...]).astype(BF16)
            rep_a[:, slot] = rep.reshape(NJ, NZ, LS)
    j_rep.start()
    rep_b[pl.ds(j, 1)] = rep_a[pl.ds(j, 1)]
    with jax.named_scope("wait_halo"):
        halo_right.wait_recv()
        halo_left.wait_recv()
        loaded("near", "nb")
    with jax.named_scope("near"):
        first = jnp.where(g > 0, 1.0, 0.0)
        last = jnp.where(g < NX * NCELL - 1, 1.0, 0.0)
        win[pl.ds(0, HW), :] = jnp.where(first > 0.5, halo[0].astype(F32), 0.0).astype(BF16)
        win[pl.ds(HW + LC, HW), :] = jnp.where(last > 0.5, halo[1].astype(F32), 0.0).astype(BF16)
        win[pl.ds(2 * HW + LC, WIN - 2 * HW - LC), :] = jnp.zeros((WIN - 2 * HW - LC, VX), BF16)
        idx_pad[...] = jnp.zeros((32, 128), F32)
        idx_pad[pl.ds(0, NN), pl.ds(0, HALF)] = near_t[...].astype(F32)
        slots = jnp.transpose(idx_pad[...])[:HALF]
        lane_w = iota((HALF, WIN), 1).astype(F32)
        window = win[...]
        for n in range(NN):
            pick = onehot(slots[:, n : n + 1] == lane_w)
            gathered[n] = dot(pick, window).astype(BF16)
        near = jnp.zeros((HALF, VX), F32)
        for n in range(NN):
            near = near + dot(gathered[n], nb[n])

    with jax.named_scope("wait_j_tree"):
        j_tree.wait_recv()
    with jax.named_scope("section_rows"):
        for yy in range(NY):
            for cc in range(2):
                up0[cc, pl.ds(32 + yy, NZ, stride=NY), :] = all_c[2 * yy + cc]
    x_right.start()
    x_left.start()

    with jax.named_scope("wait_j_rep"):
        j_rep.wait_recv()
    with jax.named_scope("regroup_replies"):
        f_rows[...] = rep_b[...].astype(F32).reshape(NJ * 64, LS)
        for zz in range(NZ):
            blocks = [f_rows[pl.ds(slot * NZ + zz, NJ, stride=64), :] for slot in range(CAP)]
            rep_c[zz] = jnp.concatenate(blocks, axis=0).astype(BF16)
    with jax.named_scope("start_z_rep"):
        z_rep.start()
    rep_d[pl.ds(z, 1)] = rep_c[pl.ds(z, 1)]

    with jax.named_scope("wait_z_cur"):
        z_cur.wait_recv()
    with jax.named_scope("regroup_currents"):
        f_rows[...] = in_cur[...].astype(F32).reshape(NZ * 32, LS)
        for jj in range(NJ):
            for slot in range(CAP):
                block = f_rows[pl.ds(slot * NJ + jj, NZ, stride=32), :]
                mid_cur[jj, slot] = block.astype(BF16)
    j_cur.start()
    all_cur[pl.ds(j, 1)] = mid_cur[pl.ds(j, 1)]

    with jax.named_scope("wait_x"):
        x_right.wait_recv()
        x_left.wait_recv()
    loaded("tab")
    tab_copy.wait_recv()
    with jax.named_scope("tree"):
        up0[:, pl.ds(0, 32), :] = jnp.where(x > 0, xrows[0], 0.0)
        up0[:, pl.ds(96, 32), :] = jnp.where(x < NX - 1, xrows[1], 0.0)
        ups = [up0, up1, up2, up3]
        waves = []
        for h in range(2):

            def entry(level, number):
                return tabs[h, level, pl.ds(number, 1), :]

            for level in range(3):
                count = 64 >> level
                even = ups[level][h, pl.ds(0, count, stride=2), :]
                odd = ups[level][h, pl.ds(1, count, stride=2), :]
                ups[level + 1][h] = entry(level, 4) * even + entry(level, 5) * odd
            terms = []
            for level in range(4):
                at = (32 + cell) >> level
                is_odd = (at & 1) == 1

                def row(offset):
                    return ups[level][h, pl.ds(at + offset, 1), :]

                term = jnp.where(is_odd, entry(level, 0) * row(-3), 0.0)
                term = term + entry(level, 1) * row(-2)
                term = term + entry(level, 2) * row(2)
                term = term + jnp.where(is_odd, 0.0, entry(level, 3) * row(3))
                terms.append(term)
            down = terms[3]
            for level in (2, 1, 0):
                is_odd = (((32 + cell) >> level) & 1) == 1
                down = terms[level] + jnp.where(is_odd, entry(level, 7), entry(level, 6)) * down
            waves.append(down)

    loaded("lin", "vrec", "srec")
    lin_copy.wait_recv()
    with jax.named_scope("far"):
        far_volume = jnp.zeros((HALF, VX), F32)
        far_surface = jnp.zeros((64, LS), F32)
        for h in range(2):
            wave = waves[h]
            leaf_own = lins[h, pl.ds(pl.multiple_of(c * HALF, 32), HALF), :].astype(F32)
            incoming = (leaf_own * wave).astype(BF16)
            far_volume = far_volume + dot(incoming, vrec[pl.ds(h * KH, KH), :])
            leaf_all = dot(host_t, lins[h], 0, 0)
            leaf_here = jnp.where(c == 0, leaf_all[:64], leaf_all[64:])
            incoming = (leaf_here * wave).astype(BF16)
            far_surface = far_surface + dot(incoming, srec[pl.ds(h * KH, KH), :])
    with jax.named_scope("wait_j_cur"):
        j_cur.wait_recv()
    with jax.named_scope("coupled_volume"):
        sums = jnp.zeros((KINDS * HALF, LS), F32)
        for slot in range(CAP):
            sums = sums + dot(picks[slot], all_cur[:, slot].reshape(LS, LS), 0, 0)
        high = sums.astype(BF16)
        low = (sums - high.astype(F32)).astype(BF16)
        coupled = jnp.zeros((HALF, VX), F32)
        for kind in range(KINDS):
            part = slice(kind * HALF, (kind + 1) * HALF)
            coupled = coupled + dot(high[part], sv[kind]) + dot(low[part], sv[kind])

    with jax.named_scope("volume_out"):
        field = vf[pl.ds(pl.multiple_of(c * HALF, 32), HALF), :].astype(F32)
        vout[...] = field + near + far_volume + coupled

    with jax.named_scope("wait_sends"):
        for exchange in (z_info, z_cur, z_tree, j_info, j_cur, j_rep, j_tree):
            exchange.wait_send()
        for copy in (lin_copy, tab_copy, halo_right, halo_left, x_right, x_left):
            copy.wait_send()
    with jax.named_scope("wait_z_rep"):
        z_rep.wait_recv()
    with jax.named_scope("coupled_surface"):
        back = rep_d[...].astype(F32)
        sublane64 = iota((64, LS), 0)
        total = far_surface
        for slot in range(CAP):
            pick = onehot(pt[0, pl.ds(slot, 1), :] == sublane64)
            mine = back[:, slot * NJ : (slot + 1) * NJ, :].reshape(LS, LS).astype(BF16)
            total = total + dot(pick, mine)
        sout[...] = total

    z_rep.wait_send()


def on_device(
    volume_field, contrast_id, contrast, near_index, near_blocks, vol_radiation, surf_radiation,
    vol_receive, surf_receive, surface_current, surf_host, leaf_out, leaf_in, level_tables,
    sv_blocks, pair_table,
):
    inputs = (
        volume_field, contrast_id, contrast, near_index.T, near_blocks, vol_radiation,
        surf_radiation, vol_receive, surf_receive, surface_current, surf_host.reshape(1, LS),
        leaf_out, leaf_in, level_tables, sv_blocks, jnp.transpose(pair_table, (2, 1, 0)),
    )
    hbm = pl.BlockSpec(memory_space=pltpu.HBM)
    vmem = pl.BlockSpec(memory_space=pltpu.VMEM)
    specs = [hbm] * 16
    shapes = (jax.ShapeDtypeStruct((HALF, VX), F32), jax.ShapeDtypeStruct((64, LS), F32))
    return pl.pallas_call(
        kernel,
        out_shape=shapes,
        in_specs=specs,
        out_specs=(vmem, vmem),
        scratch_shapes=[
            pltpu.VMEM((LC, VX), BF16),
            pltpu.VMEM((LC, VX), jnp.int32),
            pltpu.SMEM((16,), F32),
            pltpu.VMEM((NN, HALF), jnp.int32),
            pltpu.VMEM((NN, VX, VX), BF16),
            pltpu.VMEM((VX, KH), BF16),
            pltpu.VMEM((LS, KH), BF16),
            pltpu.VMEM((2 * KH, VX), BF16),
            pltpu.VMEM((2 * KH, LS), BF16),
            pltpu.VMEM((LS, LS), BF16),
            pltpu.VMEM((1, LS), jnp.int32),
            pltpu.VMEM((LC, KH), BF16),
            pltpu.VMEM((KINDS, LS, VX), BF16),
            pltpu.VMEM((3, CAP, LS), jnp.int32),
            pltpu.VMEM((WIN, VX), BF16),
            pltpu.VMEM((2, HW, VX), BF16),
            pltpu.VMEM((NZ, 1, LS), F32),
            pltpu.VMEM((NZ, 1, LS), F32),
            pltpu.VMEM((NZ, LS), F32),
            pltpu.VMEM((NJ, NZ, LS), F32),
            pltpu.VMEM((1, KH), F32),
            pltpu.VMEM((NZ, 1, KH), F32),
            pltpu.VMEM((NZ, KH), F32),
            pltpu.VMEM((NJ, NZ, KH), F32),
            pltpu.VMEM((NZ, 32, LS), BF16),
            pltpu.VMEM((NZ, 32, LS), BF16),
            pltpu.VMEM((512, LS), F32),
            pltpu.VMEM((NJ, CAP, NZ, LS), BF16),
            pltpu.VMEM((NJ, CAP, NZ, LS), BF16),
            pltpu.VMEM((KINDS * HALF, LS), BF16),
            pltpu.VMEM((NJ, CAP, NZ, LS), BF16),
            pltpu.VMEM((NJ, CAP, NZ, LS), BF16),
            pltpu.VMEM((NZ, 32, LS), BF16),
            pltpu.VMEM((NZ, 32, LS), BF16),
            pltpu.VMEM((2, 128, KH), F32),
            pltpu.VMEM((2, 2, 32, KH), F32),
            pltpu.VMEM((2, 64, KH), F32),
            pltpu.VMEM((2, 32, KH), F32),
            pltpu.VMEM((2, 16, KH), F32),
            pltpu.VMEM((2, LC, KH), BF16),
            pltpu.VMEM((2, 4, 8, KH), F32),
            pltpu.VMEM((32, 128), F32),
            pltpu.VMEM((NN, HALF, VX), BF16),
            pltpu.SemaphoreType.DMA((4,)),
            pltpu.SemaphoreType.DMA((4,)),
            pltpu.SemaphoreType.DMA((4,)),
            pltpu.SemaphoreType.DMA((4,)),
            pltpu.SemaphoreType.DMA((6,)),
            pltpu.SemaphoreType.DMA((6,)),
            pltpu.SemaphoreType.DMA((16,)),
        ],
        compiler_params=pltpu.CompilerParams(
            collective_id=0, has_side_effects=True, vmem_limit_bytes=40 * 1024 * 1024
        ),
    )(*[pltpu.with_memory_space_constraint(array, pltpu.HBM) for array in inputs])


def solution(mesh):
    in_specs = (
        P(("sec", "cell"), None),
        P(("sec", "cell"), None),
        P(),
        P(("sec", "cell", "dir"), None),
        P(),
        P(None, "dir"),
        P(None, "dir"),
        P(),
        P(),
        P(("sec", "cell"), None),
        P(("sec", "cell")),
        P(None, "dir"),
        P(None, "dir"),
        P(None, None, "dir"),
        P(),
        P(("sec", "cell", "dir"), None, None),
    )
    out_specs = (P(("sec", "cell", "dir"), None), P(("sec", "cell", "dir"), None))
    return jax.shard_map(
        on_device, mesh=mesh, in_specs=in_specs, out_specs=out_specs, check_vma=False
    )
```

```python
import jax
import jax.numpy as jnp
from jax import lax
from jax.experimental import pallas as pl
from jax.experimental.pallas import tpu as pltpu
from jax.sharding import PartitionSpec as P

MESH = pl.DeviceIdType.MESH
F32 = jnp.float32
BF16 = jnp.bfloat16

CUR_AT = 1

NX = 4
NZ = 16
NY = 4
NJ = 8
NCELL = NZ * NY
CAP = 4
KINDS = 4
LC = 192
HALF = 96
LS = 128
HW = 48
NN = 27
VX = 256
KH = 128
WIN = 384


def dot(a, b, ca=1, cb=0):
    return lax.dot_general(a, b, (((ca,), (cb,)), ((), ())), preferred_element_type=F32)


def onehot(mask):
    return jnp.where(mask, 1.0, 0.0).astype(BF16)


def iota(shape, dim):
    return lax.broadcasted_iota(jnp.int32, shape, dim)


class Exchange:
    def __init__(self, count, me, device, src, dst, send, recv):
        self.count, self.me, self.device = count, me, device
        self.src, self.dst, self.send, self.recv = src, dst, send, recv

    def start(self):
        def body(step, carry):
            low = lax.div(self.count + 1 - step, 2)
            offset = jnp.where(lax.rem(step, 2) == 1, low, self.count - low)
            target = lax.rem(self.me + offset, self.count)
            pltpu.make_async_remote_copy(
                src_ref=self.src(target),
                dst_ref=self.dst.at[self.me],
                send_sem=self.send,
                recv_sem=self.recv,
                device_id=self.device(target),
                device_id_type=MESH,
            ).start()
            return carry

        lax.fori_loop(1, self.count, body, 0)

    def offset(self, step):
        low = (self.count + 1 - step) // 2
        return low if step % 2 == 1 else self.count - low

    def start_each(self, recv):
        for step in range(1, self.count):
            target = lax.rem(self.me + self.offset(step), self.count)
            pltpu.make_async_remote_copy(
                src_ref=self.src(target),
                dst_ref=self.dst.at[self.me],
                send_sem=self.send,
                recv_sem=recv.at[step],
                device_id=self.device(target),
                device_id_type=MESH,
            ).start()

    def wait_one(self, recv, step):
        source = lax.rem(self.me + self.count - self.offset(step), self.count)
        pltpu.make_async_remote_copy(
            src_ref=self.dst.at[source],
            dst_ref=self.dst.at[source],
            send_sem=self.send,
            recv_sem=recv.at[step],
            device_id=self.device(source),
            device_id_type=MESH,
        ).wait_recv()
        return source

    def all_blocks(self):
        blocks = self.dst.at[pl.ds(0, self.count - 1)]
        return pltpu.make_async_remote_copy(
            src_ref=blocks,
            dst_ref=blocks,
            send_sem=self.send,
            recv_sem=self.recv,
            device_id=self.device(lax.rem(self.me + 1, self.count)),
            device_id_type=MESH,
        )

    def wait_recv(self):
        self.all_blocks().wait_recv()

    def wait_send(self):
        self.all_blocks().wait_send()


def kernel(
    vf_in, cid_in, con_in, near_in, nb_in, vrad_in, srad_in, vrec_in, srec_in, cur_in, host_in,
    lout_in, lin_in, tab_in, sv_in, pt_in,
    vout, sout,
    vf, cid, con, near_t, nb, vrad, srad, vrec, srec, cur, host, lout, sv, pt, win, halo, msg, in_info, mid_info, all_info, crow, in_c, mid_c, all_c,
    msg_cur, in_cur, f_rows, mid_cur, all_cur,
    table, own_rows, near_rows, rep_c, rep_d,
    up0, xrows, up1, up2, up3,
    lins, tabs, idx_pad, gathered,
    z_send, z_recv, j_send, j_recv, p_send, p_recv, own_sem, load_sem,
):
    x = lax.axis_index("sec")
    cell = lax.axis_index("cell")
    c = lax.axis_index("dir")
    z = lax.div(cell, NY)
    y = lax.rem(cell, NY)
    j = y * 2 + c
    g = x * NCELL + cell

    loads = {}
    order = [
        ("pt", pt_in, pt), ("cur", cur_in, cur), ("cid", cid_in, cid), ("vf", vf_in, vf),
        ("con", con_in, con), ("vrad", vrad_in, vrad), ("srad", srad_in, srad),
        ("host", host_in, host), ("lout", lout_in, lout), ("sv", sv_in, sv),
        ("near", near_in, near_t), ("lin", lin_in, lins.at[c]), ("tab", tab_in, tabs.at[c]),
        ("nb", nb_in, nb), ("vrec", vrec_in, vrec), ("srec", srec_in, srec),
    ]
    for number, (name, src, dst) in enumerate(order):
        loads[name] = pltpu.make_async_copy(src, dst, load_sem.at[number])
    loads["pt"].start()

    def loaded(*names):
        for name in names:
            loads[name].wait()

    def z_device(other):
        return (x, other * NY + y, c)

    def j_device(other):
        return (x, z * NY + lax.div(other, 2), lax.rem(other, 2))

    def g_device(step):
        other = lax.rem(g + step + NX * NCELL, NX * NCELL)
        return (lax.div(other, NCELL), lax.rem(other, NCELL), c)

    def x_device(step):
        return (lax.rem(x + step + NX, NX), cell, c)

    barrier = pltpu.get_barrier_semaphore()

    def greet(device):
        pl.semaphore_signal(barrier, inc=1, device_id=device, device_id_type=MESH)

    def greet_z(step, carry):
        greet(z_device(lax.rem(z + step, NZ)))
        return carry

    def greet_j(step, carry):
        greet(j_device(lax.rem(j + step, NJ)))
        return carry

    lax.fori_loop(1, NZ, greet_z, 0)
    lax.fori_loop(1, NJ, greet_j, 0)
    for step in (-1, 1):
        greet(g_device(step))
        greet(x_device(step))
    for name in loads:
        if name != "pt":
            loads[name].start()

    z_info = Exchange(NZ, z, z_device, lambda t: msg.at[t], in_info, z_send.at[0], z_recv.at[0])
    z_cur = Exchange(NZ, z, z_device, lambda t: msg_cur.at[t], in_cur, z_send.at[1], z_recv.at[1])
    z_rep = Exchange(NZ, z, z_device, lambda t: rep_c.at[t], rep_d, z_send.at[2], z_recv.at[2])
    z_tree = Exchange(NZ, z, z_device, lambda t: crow, in_c, z_send.at[3], z_recv.at[3])
    j_info = Exchange(NJ, j, j_device, lambda t: mid_info, all_info, j_send.at[0], j_recv.at[0])
    j_cur = Exchange(NJ, j, j_device, lambda t: mid_cur.at[t], all_cur, j_send.at[1], j_recv.at[1])
    j_own = Exchange(NJ, j, j_device, lambda t: own_rows, near_rows, j_send.at[2], j_recv.at[2])
    j_tree = Exchange(NJ, j, j_device, lambda t: mid_c, all_c, j_send.at[3], j_recv.at[3])

    def pair_copy(number, src, dst, device):
        return pltpu.make_async_remote_copy(
            src_ref=src,
            dst_ref=dst,
            send_sem=p_send.at[number],
            recv_sem=p_recv.at[number],
            device_id=device,
            device_id_type=MESH,
        )

    other_core = (x, cell, 1 - c)
    lin_copy = pair_copy(0, lin_in, lins.at[c], other_core)
    tab_copy = pair_copy(1, tab_in, tabs.at[c], other_core)
    halo_right = pair_copy(2, win.at[pl.ds(LC, HW)], halo.at[0], g_device(1))
    halo_left = pair_copy(3, win.at[pl.ds(HW, HW)], halo.at[1], g_device(-1))
    x_right = pair_copy(4, up0.at[:, pl.ds(NCELL, 32)], xrows.at[0], x_device(1))
    x_left = pair_copy(5, up0.at[:, pl.ds(32, 32)], xrows.at[1], x_device(-1))

    loaded("pt")
    with jax.named_scope("pairs_out"):
        rows = [pt[f].astype(F32) for f in range(3)]
        rows = jnp.concatenate(rows + [jnp.zeros((CAP, LS), F32)], axis=0)
        columns = jnp.transpose(rows)
        lane = iota((LS, LS), 1)
        row_low = iota((LS, LS), 0) & (NJ - 1)
        info = jnp.zeros((LS, LS), F32)
        for slot in range(CAP):
            for field in range(2):
                hit = lane == row_low + (field * 32 + slot * NJ)
                info = info + jnp.where(hit, columns[:, 4 + 4 * field + slot][:, None], 0.0)
        spread = onehot((iota((NZ, LS), 1) >> 3) == iota((NZ, LS), 0))
        info = dot(spread, info.astype(BF16))
        for t in range(NZ):
            msg[t] = info[t : t + 1]
    loaded("cid", "vf", "con")
    with jax.named_scope("weighted"):
        ids = cid[...]
        scale = jnp.zeros((LC, VX), F32)
        for m in range(16):
            scale = jnp.where(ids == m, con[m], scale)
        win[pl.ds(HW, LC), :] = (vf[...].astype(F32) * scale).astype(BF16)
        own_rows[...] = win[pl.ds(pl.multiple_of(HW + c * HALF, 16), HALF), :]

    loaded("vrad", "cur", "srad", "host", "lout")
    with jax.named_scope("coarse"):
        weighted = win[pl.ds(HW, LC), :]
        outgoing = dot(weighted, vrad[...])
        surf_waves = dot(cur[...], srad[...])
        host_t = onehot(host[...] == iota((LC, LS), 0))
        leaf = lout[...]
        leaf_surf = dot(host_t, leaf, 0, 0)
        coarse = jnp.sum(leaf.astype(F32) * outgoing, axis=0, keepdims=True)
        coarse = coarse + jnp.sum(leaf_surf * surf_waves, axis=0, keepdims=True)
        crow[...] = coarse
    with jax.named_scope("barrier"):
        pl.semaphore_wait(barrier, (NZ - 1) + (NJ - 1) + 4)
    with jax.named_scope("start_z_info"):
        z_info.start()
    with jax.named_scope("start_j_own"):
        j_own.start_each(own_sem)
    in_info[pl.ds(z, 1)] = msg[pl.ds(z, 1)]
    near_rows[pl.ds(j, 1)] = own_rows[...][None]

    with jax.named_scope("start_z_tree"):
        z_tree.start()
        halo_right.start()
        halo_left.start()
        lin_copy.start()
        tab_copy.start()
    in_c[pl.ds(z, 1)] = crow[...][None]

    with jax.named_scope("currents_out"):
        own = cur[pl.ds(pl.multiple_of(c * 64, 64), 64), :]
        lane64 = iota((LS, 64), 1).astype(F32)
        parts = []
        for slot in range(CAP):
            pick = onehot(columns[:, slot : slot + 1] == lane64)
            parts.append(dot(pick, own).reshape(NZ, NJ, LS))
        msg_cur[...] = jnp.concatenate(parts, axis=1).astype(BF16)

    in_cur[pl.ds(z, 1)] = msg_cur[pl.ds(z, 1)]

    if CUR_AT == 1:
        with jax.named_scope("start_z_cur"):
            z_cur.start()

    loaded("sv")
    with jax.named_scope("reply_table"):

        def fill(owner, rows):
            for kind in range(KINDS):
                block = dot(rows, sv[kind], 1, 1).astype(BF16)
                table[pl.ds(owner, 1), pl.ds(kind * HALF, HALF), :] = block[None]

        fill(j, own_rows[...])
        for step in range(1, NJ):
            owner = j_own.wait_one(own_sem, step)
            fill(owner, near_rows[pl.ds(owner, 1)].reshape(HALF, VX))
    with jax.named_scope("wait_z_info"):
        z_info.wait_recv()
    for t in range(NZ):
        mid_info[pl.ds(t, 1), :] = in_info[t]
    with jax.named_scope("start_j_info"):
        j_info.start()
    all_info[pl.ds(j, 1)] = mid_info[...][None]
    if CUR_AT == 2:
        with jax.named_scope("start_z_cur"):
            z_cur.start()
    with jax.named_scope("replies"):
        lane384 = iota((NZ, KINDS * HALF), 1).astype(F32)
        codes = mid_info[...]
        codes = codes + HALF * pltpu.roll(codes, LS - 32, 1)
        for jj in range(NJ):
            picks = []
            for slot in range(CAP):
                at = slot * NJ + jj
                picks.append(jnp.where(codes[:, at : at + 1] == lane384, 1.0, 0.0))
            pick = jnp.concatenate(picks, axis=0).astype(BF16)
            f_rows[pl.ds(jj * 64, 64), :] = dot(pick, table[jj])
    with jax.named_scope("regroup_replies"):
        for zz in range(NZ):
            blocks = [f_rows[pl.ds(slot * NZ + zz, NJ, stride=64), :] for slot in range(CAP)]
            rep_c[zz] = jnp.concatenate(blocks, axis=0).astype(BF16)
    with jax.named_scope("start_z_rep"):
        z_rep.start()
    rep_d[pl.ds(z, 1)] = rep_c[pl.ds(z, 1)]

    with jax.named_scope("wait_z_tree"):
        z_tree.wait_recv()
    for t in range(NZ):
        mid_c[pl.ds(t, 1), :] = in_c[t]
    j_tree.start()
    all_c[pl.ds(j, 1)] = mid_c[...][None]

    with jax.named_scope("wait_halo"):
        halo_right.wait_recv()
        halo_left.wait_recv()
        loaded("near", "nb")
    with jax.named_scope("near"):
        first = jnp.where(g > 0, 1.0, 0.0)
        last = jnp.where(g < NX * NCELL - 1, 1.0, 0.0)
        win[pl.ds(0, HW), :] = jnp.where(first > 0.5, halo[0].astype(F32), 0.0).astype(BF16)
        win[pl.ds(HW + LC, HW), :] = jnp.where(last > 0.5, halo[1].astype(F32), 0.0).astype(BF16)
        win[pl.ds(2 * HW + LC, WIN - 2 * HW - LC), :] = jnp.zeros((WIN - 2 * HW - LC, VX), BF16)
        idx_pad[...] = jnp.zeros((32, 128), F32)
        idx_pad[pl.ds(0, NN), pl.ds(0, HALF)] = near_t[...].astype(F32)
        slots = jnp.transpose(idx_pad[...])[:HALF]
        lane_w = iota((HALF, WIN), 1).astype(F32)
        window = win[...]
        for n in range(NN):
            pick = onehot(slots[:, n : n + 1] == lane_w)
            gathered[n] = dot(pick, window).astype(BF16)
        near = jnp.zeros((HALF, VX), F32)
        for n in range(NN):
            near = near + dot(gathered[n], nb[n])

    with jax.named_scope("wait_j_tree"):
        j_tree.wait_recv()
    with jax.named_scope("section_rows"):
        for yy in range(NY):
            for cc in range(2):
                up0[cc, pl.ds(32 + yy, NZ, stride=NY), :] = all_c[2 * yy + cc]
    x_right.start()
    x_left.start()

    with jax.named_scope("wait_z_cur"):
        z_cur.wait_recv()
    with jax.named_scope("regroup_currents"):
        f_rows[...] = in_cur[...].astype(F32).reshape(NZ * 32, LS)
        for jj in range(NJ):
            for slot in range(CAP):
                block = f_rows[pl.ds(slot * NJ + jj, NZ, stride=32), :]
                mid_cur[jj, slot] = block.astype(BF16)
    j_cur.start()
    all_cur[pl.ds(j, 1)] = mid_cur[pl.ds(j, 1)]

    with jax.named_scope("wait_x"):
        x_right.wait_recv()
        x_left.wait_recv()
    loaded("tab")
    tab_copy.wait_recv()
    with jax.named_scope("tree"):
        up0[:, pl.ds(0, 32), :] = jnp.where(x > 0, xrows[0], 0.0)
        up0[:, pl.ds(96, 32), :] = jnp.where(x < NX - 1, xrows[1], 0.0)
        ups = [up0, up1, up2, up3]
        waves = []
        for h in range(2):

            def entry(level, number):
                return tabs[h, level, pl.ds(number, 1), :]

            for level in range(3):
                count = 64 >> level
                even = ups[level][h, pl.ds(0, count, stride=2), :]
                odd = ups[level][h, pl.ds(1, count, stride=2), :]
                ups[level + 1][h] = entry(level, 4) * even + entry(level, 5) * odd
            terms = []
            for level in range(4):
                at = (32 + cell) >> level
                is_odd = (at & 1) == 1

                def row(offset):
                    return ups[level][h, pl.ds(at + offset, 1), :]

                term = jnp.where(is_odd, entry(level, 0) * row(-3), 0.0)
                term = term + entry(level, 1) * row(-2)
                term = term + entry(level, 2) * row(2)
                term = term + jnp.where(is_odd, 0.0, entry(level, 3) * row(3))
                terms.append(term)
            down = terms[3]
            for level in (2, 1, 0):
                is_odd = (((32 + cell) >> level) & 1) == 1
                down = terms[level] + jnp.where(is_odd, entry(level, 7), entry(level, 6)) * down
            waves.append(down)

    loaded("lin", "vrec", "srec")
    lin_copy.wait_recv()
    with jax.named_scope("far"):
        far_volume = jnp.zeros((HALF, VX), F32)
        far_surface = jnp.zeros((64, LS), F32)
        for h in range(2):
            wave = waves[h]
            leaf_own = lins[h, pl.ds(pl.multiple_of(c * HALF, 32), HALF), :].astype(F32)
            incoming = (leaf_own * wave).astype(BF16)
            far_volume = far_volume + dot(incoming, vrec[pl.ds(h * KH, KH), :])
            leaf_all = dot(host_t, lins[h], 0, 0)
            leaf_here = jnp.where(c == 0, leaf_all[:64], leaf_all[64:])
            incoming = (leaf_here * wave).astype(BF16)
            far_surface = far_surface + dot(incoming, srec[pl.ds(h * KH, KH), :])
    with jax.named_scope("wait_j_cur"):
        j_cur.wait_recv()
    with jax.named_scope("wait_j_info"):
        j_info.wait_recv()
    with jax.named_scope("coupled_volume"):
        codes = pltpu.roll(all_info[...].reshape(LS, LS), lax.rem(LS - j, LS), 1)
        lane384 = iota((LS, KINDS * HALF), 1).astype(F32)
        picks = []
        for slot in range(CAP):
            at = slot * NJ
            code = codes[:, at : at + 1] + HALF * codes[:, 32 + at : 33 + at]
            picks.append(onehot(code == lane384))
        sums = jnp.zeros((KINDS * HALF, LS), F32)
        for slot in range(CAP):
            sums = sums + dot(picks[slot], all_cur[:, slot].reshape(LS, LS), 0, 0)
        high = sums.astype(BF16)
        low = (sums - high.astype(F32)).astype(BF16)
        coupled = jnp.zeros((HALF, VX), F32)
        for kind in range(KINDS):
            part = slice(kind * HALF, (kind + 1) * HALF)
            coupled = coupled + dot(high[part], sv[kind]) + dot(low[part], sv[kind])

    with jax.named_scope("volume_out"):
        field = vf[pl.ds(pl.multiple_of(c * HALF, 32), HALF), :].astype(F32)
        vout[...] = field + near + far_volume + coupled

    with jax.named_scope("wait_sends"):
        for exchange in (z_info, z_cur, z_tree, j_info, j_cur, j_own, j_tree):
            exchange.wait_send()
        for copy in (lin_copy, tab_copy, halo_right, halo_left, x_right, x_left):
            copy.wait_send()
    with jax.named_scope("wait_z_rep"):
        z_rep.wait_recv()
    with jax.named_scope("coupled_surface"):
        back = rep_d[...].astype(F32)
        sublane64 = iota((64, LS), 0)
        total = far_surface
        for slot in range(CAP):
            pick = onehot(pt[0, pl.ds(slot, 1), :] == sublane64)
            mine = back[:, slot * NJ : (slot + 1) * NJ, :].reshape(LS, LS).astype(BF16)
            total = total + dot(pick, mine)
        sout[...] = total

    z_rep.wait_send()


def on_device(
    volume_field, contrast_id, contrast, near_index, near_blocks, vol_radiation, surf_radiation,
    vol_receive, surf_receive, surface_current, surf_host, leaf_out, leaf_in, level_tables,
    sv_blocks, pair_table,
):
    inputs = (
        volume_field, contrast_id, contrast, near_index.T, near_blocks, vol_radiation,
        surf_radiation, vol_receive, surf_receive, surface_current, surf_host.reshape(1, LS),
        leaf_out, leaf_in, level_tables, sv_blocks, jnp.transpose(pair_table, (2, 1, 0)),
    )
    hbm = pl.BlockSpec(memory_space=pltpu.HBM)
    vmem = pl.BlockSpec(memory_space=pltpu.VMEM)
    specs = [hbm] * 16
    shapes = (jax.ShapeDtypeStruct((HALF, VX), F32), jax.ShapeDtypeStruct((64, LS), F32))
    return pl.pallas_call(
        kernel,
        out_shape=shapes,
        in_specs=specs,
        out_specs=(vmem, vmem),
        scratch_shapes=[
            pltpu.VMEM((LC, VX), BF16),
            pltpu.VMEM((LC, VX), jnp.int32),
            pltpu.SMEM((16,), F32),
            pltpu.VMEM((NN, HALF), jnp.int32),
            pltpu.VMEM((NN, VX, VX), BF16),
            pltpu.VMEM((VX, KH), BF16),
            pltpu.VMEM((LS, KH), BF16),
            pltpu.VMEM((2 * KH, VX), BF16),
            pltpu.VMEM((2 * KH, LS), BF16),
            pltpu.VMEM((LS, LS), BF16),
            pltpu.VMEM((1, LS), jnp.int32),
            pltpu.VMEM((LC, KH), BF16),
            pltpu.VMEM((KINDS, LS, VX), BF16),
            pltpu.VMEM((3, CAP, LS), jnp.int32),
            pltpu.VMEM((WIN, VX), BF16),
            pltpu.VMEM((2, HW, VX), BF16),
            pltpu.VMEM((NZ, 1, LS), F32),
            pltpu.VMEM((NZ, 1, LS), F32),
            pltpu.VMEM((NZ, LS), F32),
            pltpu.VMEM((NJ, NZ, LS), F32),
            pltpu.VMEM((1, KH), F32),
            pltpu.VMEM((NZ, 1, KH), F32),
            pltpu.VMEM((NZ, KH), F32),
            pltpu.VMEM((NJ, NZ, KH), F32),
            pltpu.VMEM((NZ, 32, LS), BF16),
            pltpu.VMEM((NZ, 32, LS), BF16),
            pltpu.VMEM((512, LS), F32),
            pltpu.VMEM((NJ, CAP, NZ, LS), BF16),
            pltpu.VMEM((NJ, CAP, NZ, LS), BF16),
            pltpu.VMEM((NJ, KINDS * HALF, LS), BF16),
            pltpu.VMEM((HALF, VX), BF16),
            pltpu.VMEM((NJ, HALF, VX), BF16),
            pltpu.VMEM((NZ, 32, LS), BF16),
            pltpu.VMEM((NZ, 32, LS), BF16),
            pltpu.VMEM((2, 128, KH), F32),
            pltpu.VMEM((2, 2, 32, KH), F32),
            pltpu.VMEM((2, 64, KH), F32),
            pltpu.VMEM((2, 32, KH), F32),
            pltpu.VMEM((2, 16, KH), F32),
            pltpu.VMEM((2, LC, KH), BF16),
            pltpu.VMEM((2, 4, 8, KH), F32),
            pltpu.VMEM((32, 128), F32),
            pltpu.VMEM((NN, HALF, VX), BF16),
            pltpu.SemaphoreType.DMA((4,)),
            pltpu.SemaphoreType.DMA((4,)),
            pltpu.SemaphoreType.DMA((4,)),
            pltpu.SemaphoreType.DMA((4,)),
            pltpu.SemaphoreType.DMA((6,)),
            pltpu.SemaphoreType.DMA((6,)),
            pltpu.SemaphoreType.DMA((NJ,)),
            pltpu.SemaphoreType.DMA((16,)),
        ],
        compiler_params=pltpu.CompilerParams(
            collective_id=0, has_side_effects=True, vmem_limit_bytes=40 * 1024 * 1024
        ),
    )(*[pltpu.with_memory_space_constraint(array, pltpu.HBM) for array in inputs])


def solution(mesh):
    in_specs = (
        P(("sec", "cell"), None),
        P(("sec", "cell"), None),
        P(),
        P(("sec", "cell", "dir"), None),
        P(),
        P(None, "dir"),
        P(None, "dir"),
        P(),
        P(),
        P(("sec", "cell"), None),
        P(("sec", "cell")),
        P(None, "dir"),
        P(None, "dir"),
        P(None, None, "dir"),
        P(),
        P(("sec", "cell", "dir"), None, None),
    )
    out_specs = (P(("sec", "cell", "dir"), None), P(("sec", "cell", "dir"), None))
    return jax.shard_map(
        on_device, mesh=mesh, in_specs=in_specs, out_specs=out_specs, check_vma=False
    )
```

```python
import jax
import jax.numpy as jnp
from jax import lax
from jax.experimental import pallas as pl
from jax.experimental.pallas import tpu as pltpu
from jax.sharding import PartitionSpec as P

MESH = pl.DeviceIdType.MESH
F32 = jnp.float32
BF16 = jnp.bfloat16

NX = 4
NZ = 16
NY = 4
NJ = 8
NCELL = NZ * NY
CAP = 4
KINDS = 4
LC = 192
HALF = 96
LS = 128
HW = 48
NN = 27
VX = 256
KH = 128
WIN = 384


def dot(a, b, ca=1, cb=0):
    return lax.dot_general(a, b, (((ca,), (cb,)), ((), ())), preferred_element_type=F32)


def onehot(mask):
    return jnp.where(mask, 1.0, 0.0).astype(BF16)


def iota(shape, dim):
    return lax.broadcasted_iota(jnp.int32, shape, dim)


class Exchange:
    def __init__(self, count, me, device, src, dst, send, recv):
        self.count, self.me, self.device = count, me, device
        self.src, self.dst, self.send, self.recv = src, dst, send, recv

    def start(self):
        def body(step, carry):
            low = lax.div(self.count + 1 - step, 2)
            offset = jnp.where(lax.rem(step, 2) == 1, low, self.count - low)
            target = lax.rem(self.me + offset, self.count)
            pltpu.make_async_remote_copy(
                src_ref=self.src(target),
                dst_ref=self.dst.at[self.me],
                send_sem=self.send,
                recv_sem=self.recv,
                device_id=self.device(target),
                device_id_type=MESH,
            ).start()
            return carry

        lax.fori_loop(1, self.count, body, 0)

    def offset(self, step):
        low = (self.count + 1 - step) // 2
        return low if step % 2 == 1 else self.count - low

    def start_each(self, recv):
        for step in range(1, self.count):
            target = lax.rem(self.me + self.offset(step), self.count)
            pltpu.make_async_remote_copy(
                src_ref=self.src(target),
                dst_ref=self.dst.at[self.me],
                send_sem=self.send,
                recv_sem=recv.at[step],
                device_id=self.device(target),
                device_id_type=MESH,
            ).start()

    def wait_one(self, recv, step):
        source = lax.rem(self.me + self.count - self.offset(step), self.count)
        pltpu.make_async_remote_copy(
            src_ref=self.dst.at[source],
            dst_ref=self.dst.at[source],
            send_sem=self.send,
            recv_sem=recv.at[step],
            device_id=self.device(source),
            device_id_type=MESH,
        ).wait_recv()
        return source

    def all_blocks(self):
        blocks = self.dst.at[pl.ds(0, self.count - 1)]
        return pltpu.make_async_remote_copy(
            src_ref=blocks,
            dst_ref=blocks,
            send_sem=self.send,
            recv_sem=self.recv,
            device_id=self.device(lax.rem(self.me + 1, self.count)),
            device_id_type=MESH,
        )

    def wait_recv(self):
        self.all_blocks().wait_recv()

    def wait_send(self):
        self.all_blocks().wait_send()


def kernel(
    vf_in, cid_in, con_in, near_in, nb_in, vrad_in, srad_in, vrec_in, srec_in, cur_in, host_in,
    lout_in, lin_in, tab_in, sv_in, pt_in,
    vout, sout,
    vf, cid, con, near_t, nb, vrad, srad, vrec, srec, cur, host, lout, sv, pt, win, halo, msg, in_info, mid_info, all_info, crow, in_c, mid_c, all_c,
    msg_cur, in_cur, f_rows, mid_cur, all_cur,
    table, own_rows, near_rows, rep_c, rep_d,
    up0, xrows, up1, up2, up3,
    lins, tabs, idx_pad, gathered,
    z_send, z_recv, j_send, j_recv, p_send, p_recv, own_sem, load_sem,
):
    x = lax.axis_index("sec")
    cell = lax.axis_index("cell")
    c = lax.axis_index("dir")
    z = lax.div(cell, NY)
    y = lax.rem(cell, NY)
    j = y * 2 + c
    g = x * NCELL + cell

    loads = {}
    order = [
        ("pt", pt_in, pt), ("cur", cur_in, cur), ("cid", cid_in, cid), ("vf", vf_in, vf),
        ("con", con_in, con), ("vrad", vrad_in, vrad), ("srad", srad_in, srad),
        ("host", host_in, host), ("lout", lout_in, lout), ("sv", sv_in, sv),
        ("near", near_in, near_t), ("lin", lin_in, lins.at[c]), ("tab", tab_in, tabs.at[c]),
        ("nb", nb_in, nb), ("vrec", vrec_in, vrec), ("srec", srec_in, srec),
    ]
    for number, (name, src, dst) in enumerate(order):
        loads[name] = pltpu.make_async_copy(src, dst, load_sem.at[number])
    loads["pt"].start()

    def loaded(*names):
        for name in names:
            loads[name].wait()

    def z_device(other):
        return (x, other * NY + y, c)

    def j_device(other):
        return (x, z * NY + lax.div(other, 2), lax.rem(other, 2))

    def g_device(step):
        other = lax.rem(g + step + NX * NCELL, NX * NCELL)
        return (lax.div(other, NCELL), lax.rem(other, NCELL), c)

    def x_device(step):
        return (lax.rem(x + step + NX, NX), cell, c)

    barrier = pltpu.get_barrier_semaphore()

    def greet(device):
        pl.semaphore_signal(barrier, inc=1, device_id=device, device_id_type=MESH)

    def greet_z(step, carry):
        greet(z_device(lax.rem(z + step, NZ)))
        return carry

    def greet_j(step, carry):
        greet(j_device(lax.rem(j + step, NJ)))
        return carry

    lax.fori_loop(1, NZ, greet_z, 0)
    lax.fori_loop(1, NJ, greet_j, 0)
    for step in (-1, 1):
        greet(g_device(step))
        greet(x_device(step))
    for name in loads:
        if name != "pt":
            loads[name].start()

    z_info = Exchange(NZ, z, z_device, lambda t: msg.at[t], in_info, z_send.at[0], z_recv.at[0])
    z_cur = Exchange(NZ, z, z_device, lambda t: msg_cur.at[t], in_cur, z_send.at[1], z_recv.at[1])
    z_rep = Exchange(NZ, z, z_device, lambda t: rep_c.at[t], rep_d, z_send.at[2], z_recv.at[2])
    z_tree = Exchange(NZ, z, z_device, lambda t: crow, in_c, z_send.at[3], z_recv.at[3])
    j_info = Exchange(NJ, j, j_device, lambda t: mid_info, all_info, j_send.at[0], j_recv.at[0])
    j_cur = Exchange(NJ, j, j_device, lambda t: mid_cur.at[t], all_cur, j_send.at[1], j_recv.at[1])
    j_own = Exchange(NJ, j, j_device, lambda t: own_rows, near_rows, j_send.at[2], j_recv.at[2])
    j_tree = Exchange(NJ, j, j_device, lambda t: mid_c, all_c, j_send.at[3], j_recv.at[3])

    def pair_copy(number, src, dst, device):
        return pltpu.make_async_remote_copy(
            src_ref=src,
            dst_ref=dst,
            send_sem=p_send.at[number],
            recv_sem=p_recv.at[number],
            device_id=device,
            device_id_type=MESH,
        )

    other_core = (x, cell, 1 - c)
    lin_copy = pair_copy(0, lin_in, lins.at[c], other_core)
    tab_copy = pair_copy(1, tab_in, tabs.at[c], other_core)
    halo_right = pair_copy(2, win.at[pl.ds(LC, HW)], halo.at[0], g_device(1))
    halo_left = pair_copy(3, win.at[pl.ds(HW, HW)], halo.at[1], g_device(-1))
    x_right = pair_copy(4, up0.at[:, pl.ds(NCELL, 32)], xrows.at[0], x_device(1))
    x_left = pair_copy(5, up0.at[:, pl.ds(32, 32)], xrows.at[1], x_device(-1))

    loaded("pt")
    with jax.named_scope("pairs_out"):
        rows = [pt[f].astype(F32) for f in range(3)]
        rows = jnp.concatenate(rows + [jnp.zeros((CAP, LS), F32)], axis=0)
        columns = jnp.transpose(rows)
        lane = iota((LS, LS), 1)
        row_low = iota((LS, LS), 0) & (NJ - 1)
        info = jnp.zeros((LS, LS), F32)
        for slot in range(CAP):
            for field in range(2):
                hit = lane == row_low + (field * 32 + slot * NJ)
                info = info + jnp.where(hit, columns[:, 4 + 4 * field + slot][:, None], 0.0)
        spread = onehot((iota((NZ, LS), 1) >> 3) == iota((NZ, LS), 0))
        info = dot(spread, info.astype(BF16))
        for t in range(NZ):
            msg[t] = info[t : t + 1]
    loaded("cid", "vf", "con")
    with jax.named_scope("weighted"):
        ids = cid[...]
        scale = jnp.zeros((LC, VX), F32)
        for m in range(16):
            scale = jnp.where(ids == m, con[m], scale)
        win[pl.ds(HW, LC), :] = (vf[...].astype(F32) * scale).astype(BF16)
        own_rows[...] = win[pl.ds(pl.multiple_of(HW + c * HALF, 16), HALF), :]

    loaded("vrad", "cur", "srad", "host", "lout")
    with jax.named_scope("coarse"):
        weighted = win[pl.ds(HW, LC), :]
        outgoing = dot(weighted, vrad[...])
        surf_waves = dot(cur[...], srad[...])
        host_t = onehot(host[...] == iota((LC, LS), 0))
        leaf = lout[...]
        leaf_surf = dot(host_t, leaf, 0, 0)
        coarse = jnp.sum(leaf.astype(F32) * outgoing, axis=0, keepdims=True)
        coarse = coarse + jnp.sum(leaf_surf * surf_waves, axis=0, keepdims=True)
        crow[...] = coarse
    with jax.named_scope("barrier"):
        pl.semaphore_wait(barrier, (NZ - 1) + (NJ - 1) + 4)
    with jax.named_scope("start_j_own"):
        j_own.start_each(own_sem)
    with jax.named_scope("start_z_info"):
        z_info.start()
    in_info[pl.ds(z, 1)] = msg[pl.ds(z, 1)]
    near_rows[pl.ds(j, 1)] = own_rows[...][None]

    with jax.named_scope("start_z_tree"):
        z_tree.start()
        halo_right.start()
        halo_left.start()
        lin_copy.start()
        tab_copy.start()
    in_c[pl.ds(z, 1)] = crow[...][None]

    with jax.named_scope("currents_out"):
        own = cur[pl.ds(pl.multiple_of(c * 64, 64), 64), :]
        lane64 = iota((LS, 64), 1).astype(F32)
        parts = []
        for slot in range(CAP):
            pick = onehot(columns[:, slot : slot + 1] == lane64)
            parts.append(dot(pick, own).reshape(NZ, NJ, LS))
        msg_cur[...] = jnp.concatenate(parts, axis=1).astype(BF16)

    in_cur[pl.ds(z, 1)] = msg_cur[pl.ds(z, 1)]

    with jax.named_scope("start_z_cur"):
        z_cur.start()

    loaded("sv")
    with jax.named_scope("reply_table"):

        def fill(owner, rows):
            for kind in range(KINDS):
                block = dot(rows, sv[kind], 1, 1).astype(BF16)
                table[pl.ds(owner, 1), pl.ds(kind * HALF, HALF), :] = block[None]

        fill(j, own_rows[...])
        for step in range(1, NJ):
            owner = j_own.wait_one(own_sem, step)
            fill(owner, near_rows[pl.ds(owner, 1)].reshape(HALF, VX))
    with jax.named_scope("wait_z_info"):
        z_info.wait_recv()
    for t in range(NZ):
        mid_info[pl.ds(t, 1), :] = in_info[t]
    with jax.named_scope("start_j_info"):
        j_info.start()
    all_info[pl.ds(j, 1)] = mid_info[...][None]
    with jax.named_scope("wait_z_tree"):
        z_tree.wait_recv()
    for t in range(NZ):
        mid_c[pl.ds(t, 1), :] = in_c[t]
    j_tree.start()
    all_c[pl.ds(j, 1)] = mid_c[...][None]
    with jax.named_scope("replies"):
        lane384 = iota((NZ, KINDS * HALF), 1).astype(F32)
        codes = mid_info[...]
        codes = codes + HALF * pltpu.roll(codes, LS - 32, 1)
        for jj in range(NJ):
            picks = []
            for slot in range(CAP):
                at = slot * NJ + jj
                picks.append(jnp.where(codes[:, at : at + 1] == lane384, 1.0, 0.0))
            pick = jnp.concatenate(picks, axis=0).astype(BF16)
            f_rows[pl.ds(jj * 64, 64), :] = dot(pick, table[jj])
    with jax.named_scope("regroup_replies"):
        for zz in range(NZ):
            blocks = [f_rows[pl.ds(slot * NZ + zz, NJ, stride=64), :] for slot in range(CAP)]
            rep_c[zz] = jnp.concatenate(blocks, axis=0).astype(BF16)
    with jax.named_scope("start_z_rep"):
        z_rep.start()
    rep_d[pl.ds(z, 1)] = rep_c[pl.ds(z, 1)]

    with jax.named_scope("wait_z_cur"):
        z_cur.wait_recv()
    with jax.named_scope("regroup_currents"):
        f_rows[...] = in_cur[...].astype(F32).reshape(NZ * 32, LS)
        for jj in range(NJ):
            for slot in range(CAP):
                block = f_rows[pl.ds(slot * NJ + jj, NZ, stride=32), :]
                mid_cur[jj, slot] = block.astype(BF16)
    j_cur.start()
    all_cur[pl.ds(j, 1)] = mid_cur[pl.ds(j, 1)]

    with jax.named_scope("wait_halo"):
        halo_right.wait_recv()
        halo_left.wait_recv()
        loaded("near", "nb")
    with jax.named_scope("near"):
        first = jnp.where(g > 0, 1.0, 0.0)
        last = jnp.where(g < NX * NCELL - 1, 1.0, 0.0)
        win[pl.ds(0, HW), :] = jnp.where(first > 0.5, halo[0].astype(F32), 0.0).astype(BF16)
        win[pl.ds(HW + LC, HW), :] = jnp.where(last > 0.5, halo[1].astype(F32), 0.0).astype(BF16)
        win[pl.ds(2 * HW + LC, WIN - 2 * HW - LC), :] = jnp.zeros((WIN - 2 * HW - LC, VX), BF16)
        idx_pad[...] = jnp.zeros((32, 128), F32)
        idx_pad[pl.ds(0, NN), pl.ds(0, HALF)] = near_t[...].astype(F32)
        slots = jnp.transpose(idx_pad[...])[:HALF]
        lane_w = iota((HALF, WIN), 1).astype(F32)
        window = win[...]
        for n in range(NN):
            pick = onehot(slots[:, n : n + 1] == lane_w)
            gathered[n] = dot(pick, window).astype(BF16)

    with jax.named_scope("wait_j_tree"):
        j_tree.wait_recv()
    with jax.named_scope("section_rows"):
        for yy in range(NY):
            for cc in range(2):
                up0[cc, pl.ds(32 + yy, NZ, stride=NY), :] = all_c[2 * yy + cc]
    x_right.start()
    x_left.start()

    with jax.named_scope("near_blocks"):
        near = jnp.zeros((HALF, VX), F32)
        for n in range(NN):
            near = near + dot(gathered[n], nb[n])

    with jax.named_scope("wait_j_cur"):
        j_cur.wait_recv()
    with jax.named_scope("wait_j_info"):
        j_info.wait_recv()
    with jax.named_scope("coupled_volume"):
        codes = pltpu.roll(all_info[...].reshape(LS, LS), lax.rem(LS - j, LS), 1)
        lane384 = iota((LS, KINDS * HALF), 1).astype(F32)
        picks = []
        for slot in range(CAP):
            at = slot * NJ
            code = codes[:, at : at + 1] + HALF * codes[:, 32 + at : 33 + at]
            picks.append(onehot(code == lane384))
        sums = jnp.zeros((KINDS * HALF, LS), F32)
        for slot in range(CAP):
            sums = sums + dot(picks[slot], all_cur[:, slot].reshape(LS, LS), 0, 0)
        high = sums.astype(BF16)
        low = (sums - high.astype(F32)).astype(BF16)
        coupled = jnp.zeros((HALF, VX), F32)
        for kind in range(KINDS):
            part = slice(kind * HALF, (kind + 1) * HALF)
            coupled = coupled + dot(high[part], sv[kind]) + dot(low[part], sv[kind])

    with jax.named_scope("wait_x"):
        x_right.wait_recv()
        x_left.wait_recv()
    loaded("tab")
    tab_copy.wait_recv()
    with jax.named_scope("tree"):
        up0[:, pl.ds(0, 32), :] = jnp.where(x > 0, xrows[0], 0.0)
        up0[:, pl.ds(96, 32), :] = jnp.where(x < NX - 1, xrows[1], 0.0)
        ups = [up0, up1, up2, up3]
        waves = []
        for h in range(2):

            def entry(level, number):
                return tabs[h, level, pl.ds(number, 1), :]

            for level in range(3):
                count = 64 >> level
                even = ups[level][h, pl.ds(0, count, stride=2), :]
                odd = ups[level][h, pl.ds(1, count, stride=2), :]
                ups[level + 1][h] = entry(level, 4) * even + entry(level, 5) * odd
            terms = []
            for level in range(4):
                at = (32 + cell) >> level
                is_odd = (at & 1) == 1

                def row(offset):
                    return ups[level][h, pl.ds(at + offset, 1), :]

                term = jnp.where(is_odd, entry(level, 0) * row(-3), 0.0)
                term = term + entry(level, 1) * row(-2)
                term = term + entry(level, 2) * row(2)
                term = term + jnp.where(is_odd, 0.0, entry(level, 3) * row(3))
                terms.append(term)
            down = terms[3]
            for level in (2, 1, 0):
                is_odd = (((32 + cell) >> level) & 1) == 1
                down = terms[level] + jnp.where(is_odd, entry(level, 7), entry(level, 6)) * down
            waves.append(down)

    loaded("lin", "vrec", "srec")
    lin_copy.wait_recv()
    with jax.named_scope("far"):
        far_volume = jnp.zeros((HALF, VX), F32)
        far_surface = jnp.zeros((64, LS), F32)
        for h in range(2):
            wave = waves[h]
            leaf_own = lins[h, pl.ds(pl.multiple_of(c * HALF, 32), HALF), :].astype(F32)
            incoming = (leaf_own * wave).astype(BF16)
            far_volume = far_volume + dot(incoming, vrec[pl.ds(h * KH, KH), :])
            leaf_all = dot(host_t, lins[h], 0, 0)
            leaf_here = jnp.where(c == 0, leaf_all[:64], leaf_all[64:])
            incoming = (leaf_here * wave).astype(BF16)
            far_surface = far_surface + dot(incoming, srec[pl.ds(h * KH, KH), :])
    with jax.named_scope("volume_out"):
        field = vf[pl.ds(pl.multiple_of(c * HALF, 32), HALF), :].astype(F32)
        vout[...] = field + near + far_volume + coupled

    with jax.named_scope("wait_sends"):
        for exchange in (z_info, z_cur, z_tree, j_info, j_cur, j_own, j_tree):
            exchange.wait_send()
        for copy in (lin_copy, tab_copy, halo_right, halo_left, x_right, x_left):
            copy.wait_send()
    with jax.named_scope("wait_z_rep"):
        z_rep.wait_recv()
    with jax.named_scope("coupled_surface"):
        back = rep_d[...].astype(F32)
        sublane64 = iota((64, LS), 0)
        total = far_surface
        for slot in range(CAP):
            pick = onehot(pt[0, pl.ds(slot, 1), :] == sublane64)
            mine = back[:, slot * NJ : (slot + 1) * NJ, :].reshape(LS, LS).astype(BF16)
            total = total + dot(pick, mine)
        sout[...] = total

    z_rep.wait_send()


def on_device(
    volume_field, contrast_id, contrast, near_index, near_blocks, vol_radiation, surf_radiation,
    vol_receive, surf_receive, surface_current, surf_host, leaf_out, leaf_in, level_tables,
    sv_blocks, pair_table,
):
    inputs = (
        volume_field, contrast_id, contrast, near_index.T, near_blocks, vol_radiation,
        surf_radiation, vol_receive, surf_receive, surface_current, surf_host.reshape(1, LS),
        leaf_out, leaf_in, level_tables, sv_blocks, jnp.transpose(pair_table, (2, 1, 0)),
    )
    hbm = pl.BlockSpec(memory_space=pltpu.HBM)
    vmem = pl.BlockSpec(memory_space=pltpu.VMEM)
    specs = [hbm] * 16
    shapes = (jax.ShapeDtypeStruct((HALF, VX), F32), jax.ShapeDtypeStruct((64, LS), F32))
    return pl.pallas_call(
        kernel,
        out_shape=shapes,
        in_specs=specs,
        out_specs=(vmem, vmem),
        scratch_shapes=[
            pltpu.VMEM((LC, VX), BF16),
            pltpu.VMEM((LC, VX), jnp.int32),
            pltpu.SMEM((16,), F32),
            pltpu.VMEM((NN, HALF), jnp.int32),
            pltpu.VMEM((NN, VX, VX), BF16),
            pltpu.VMEM((VX, KH), BF16),
            pltpu.VMEM((LS, KH), BF16),
            pltpu.VMEM((2 * KH, VX), BF16),
            pltpu.VMEM((2 * KH, LS), BF16),
            pltpu.VMEM((LS, LS), BF16),
            pltpu.VMEM((1, LS), jnp.int32),
            pltpu.VMEM((LC, KH), BF16),
            pltpu.VMEM((KINDS, LS, VX), BF16),
            pltpu.VMEM((3, CAP, LS), jnp.int32),
            pltpu.VMEM((WIN, VX), BF16),
            pltpu.VMEM((2, HW, VX), BF16),
            pltpu.VMEM((NZ, 1, LS), F32),
            pltpu.VMEM((NZ, 1, LS), F32),
            pltpu.VMEM((NZ, LS), F32),
            pltpu.VMEM((NJ, NZ, LS), F32),
            pltpu.VMEM((1, KH), F32),
            pltpu.VMEM((NZ, 1, KH), F32),
            pltpu.VMEM((NZ, KH), F32),
            pltpu.VMEM((NJ, NZ, KH), F32),
            pltpu.VMEM((NZ, 32, LS), BF16),
            pltpu.VMEM((NZ, 32, LS), BF16),
            pltpu.VMEM((512, LS), F32),
            pltpu.VMEM((NJ, CAP, NZ, LS), BF16),
            pltpu.VMEM((NJ, CAP, NZ, LS), BF16),
            pltpu.VMEM((NJ, KINDS * HALF, LS), BF16),
            pltpu.VMEM((HALF, VX), BF16),
            pltpu.VMEM((NJ, HALF, VX), BF16),
            pltpu.VMEM((NZ, 32, LS), BF16),
            pltpu.VMEM((NZ, 32, LS), BF16),
            pltpu.VMEM((2, 128, KH), F32),
            pltpu.VMEM((2, 2, 32, KH), F32),
            pltpu.VMEM((2, 64, KH), F32),
            pltpu.VMEM((2, 32, KH), F32),
            pltpu.VMEM((2, 16, KH), F32),
            pltpu.VMEM((2, LC, KH), BF16),
            pltpu.VMEM((2, 4, 8, KH), F32),
            pltpu.VMEM((32, 128), F32),
            pltpu.VMEM((NN, HALF, VX), BF16),
            pltpu.SemaphoreType.DMA((4,)),
            pltpu.SemaphoreType.DMA((4,)),
            pltpu.SemaphoreType.DMA((4,)),
            pltpu.SemaphoreType.DMA((4,)),
            pltpu.SemaphoreType.DMA((6,)),
            pltpu.SemaphoreType.DMA((6,)),
            pltpu.SemaphoreType.DMA((NJ,)),
            pltpu.SemaphoreType.DMA((16,)),
        ],
        compiler_params=pltpu.CompilerParams(
            collective_id=0, has_side_effects=True, vmem_limit_bytes=40 * 1024 * 1024
        ),
    )(*[pltpu.with_memory_space_constraint(array, pltpu.HBM) for array in inputs])


def solution(mesh):
    in_specs = (
        P(("sec", "cell"), None),
        P(("sec", "cell"), None),
        P(),
        P(("sec", "cell", "dir"), None),
        P(),
        P(None, "dir"),
        P(None, "dir"),
        P(),
        P(),
        P(("sec", "cell"), None),
        P(("sec", "cell")),
        P(None, "dir"),
        P(None, "dir"),
        P(None, None, "dir"),
        P(),
        P(("sec", "cell", "dir"), None, None),
    )
    out_specs = (P(("sec", "cell", "dir"), None), P(("sec", "cell", "dir"), None))
    return jax.shard_map(
        on_device, mesh=mesh, in_specs=in_specs, out_specs=out_specs, check_vma=False
    )
```

```python
import jax
import jax.numpy as jnp
from jax import lax
from jax.experimental import pallas as pl
from jax.experimental.pallas import tpu as pltpu
from jax.sharding import PartitionSpec as P

MESH = pl.DeviceIdType.MESH
F32 = jnp.float32
BF16 = jnp.bfloat16

NX = 4
NZ = 16
NY = 4
NJ = 8
NCELL = NZ * NY
CAP = 4
KINDS = 4
LC = 192
HALF = 96
LS = 128
HW = 48
NN = 27
VX = 256
KH = 128
WIN = 384


def dot(a, b, ca=1, cb=0):
    return lax.dot_general(a, b, (((ca,), (cb,)), ((), ())), preferred_element_type=F32)


def onehot(mask):
    return jnp.where(mask, 1.0, 0.0).astype(BF16)


def iota(shape, dim):
    return lax.broadcasted_iota(jnp.int32, shape, dim)


class Exchange:
    def __init__(self, count, me, device, src, dst, send, recv):
        self.count, self.me, self.device = count, me, device
        self.src, self.dst, self.send, self.recv = src, dst, send, recv

    def start(self):
        def body(step, carry):
            low = lax.div(self.count + 1 - step, 2)
            offset = jnp.where(lax.rem(step, 2) == 1, low, self.count - low)
            target = lax.rem(self.me + offset, self.count)
            pltpu.make_async_remote_copy(
                src_ref=self.src(target),
                dst_ref=self.dst.at[self.me],
                send_sem=self.send,
                recv_sem=self.recv,
                device_id=self.device(target),
                device_id_type=MESH,
            ).start()
            return carry

        lax.fori_loop(1, self.count, body, 0)

    def offset(self, step):
        low = (self.count + 1 - step) // 2
        return low if step % 2 == 1 else self.count - low

    def start_each(self, recv):
        for step in range(1, self.count):
            target = lax.rem(self.me + self.offset(step), self.count)
            pltpu.make_async_remote_copy(
                src_ref=self.src(target),
                dst_ref=self.dst.at[self.me],
                send_sem=self.send,
                recv_sem=recv.at[step],
                device_id=self.device(target),
                device_id_type=MESH,
            ).start()

    def wait_one(self, recv, step):
        source = lax.rem(self.me + self.count - self.offset(step), self.count)
        pltpu.make_async_remote_copy(
            src_ref=self.dst.at[source],
            dst_ref=self.dst.at[source],
            send_sem=self.send,
            recv_sem=recv.at[step],
            device_id=self.device(source),
            device_id_type=MESH,
        ).wait_recv()
        return source

    def all_blocks(self):
        blocks = self.dst.at[pl.ds(0, self.count - 1)]
        return pltpu.make_async_remote_copy(
            src_ref=blocks,
            dst_ref=blocks,
            send_sem=self.send,
            recv_sem=self.recv,
            device_id=self.device(lax.rem(self.me + 1, self.count)),
            device_id_type=MESH,
        )

    def wait_recv(self):
        self.all_blocks().wait_recv()

    def wait_send(self):
        self.all_blocks().wait_send()


def kernel(
    vf_in, cid_in, con_in, near_in, nb_in, vrad_in, srad_in, vrec_in, srec_in, cur_in, host_in,
    lout_in, lin_in, tab_in, sv_in, pt_in,
    vout, sout,
    vf, cid, con, near_t, nb, vrad, srad, vrec, srec, cur, host, lout, sv, pt, win, halo, msg, in_info, mid_info, all_info, crow, in_c, mid_c, all_c,
    msg_cur, in_cur, f_rows, mid_cur, all_cur,
    table, own_rows, near_rows, rep_c, rep_d,
    up0, xrows, up1, up2, up3,
    lins, tabs, idx_pad, gathered,
    z_send, z_recv, j_send, j_recv, p_send, p_recv, own_sem, load_sem,
):
    x = lax.axis_index("sec")
    cell = lax.axis_index("cell")
    c = lax.axis_index("dir")
    z = lax.div(cell, NY)
    y = lax.rem(cell, NY)
    j = y * 2 + c
    g = x * NCELL + cell

    loads = {}
    order = [
        ("pt", pt_in, pt), ("cur", cur_in, cur), ("cid", cid_in, cid), ("vf", vf_in, vf),
        ("con", con_in, con), ("vrad", vrad_in, vrad), ("srad", srad_in, srad),
        ("host", host_in, host), ("lout", lout_in, lout), ("sv", sv_in, sv),
        ("near", near_in, near_t), ("lin", lin_in, lins.at[c]), ("tab", tab_in, tabs.at[c]),
        ("nb", nb_in, nb), ("vrec", vrec_in, vrec), ("srec", srec_in, srec),
    ]
    for number, (name, src, dst) in enumerate(order):
        loads[name] = pltpu.make_async_copy(src, dst, load_sem.at[number])
    loads["pt"].start()

    def loaded(*names):
        for name in names:
            loads[name].wait()

    def z_device(other):
        return (x, other * NY + y, c)

    def j_device(other):
        return (x, z * NY + lax.div(other, 2), lax.rem(other, 2))

    def g_device(step):
        other = lax.rem(g + step + NX * NCELL, NX * NCELL)
        return (lax.div(other, NCELL), lax.rem(other, NCELL), c)

    def x_device(step):
        return (lax.rem(x + step + NX, NX), cell, c)

    barrier = pltpu.get_barrier_semaphore()

    def greet(device):
        pl.semaphore_signal(barrier, inc=1, device_id=device, device_id_type=MESH)

    def greet_z(step, carry):
        greet(z_device(lax.rem(z + step, NZ)))
        return carry

    def greet_j(step, carry):
        greet(j_device(lax.rem(j + step, NJ)))
        return carry

    lax.fori_loop(1, NZ, greet_z, 0)
    lax.fori_loop(1, NJ, greet_j, 0)
    for step in (-1, 1):
        greet(g_device(step))
        greet(x_device(step))
    for name in loads:
        if name != "pt":
            loads[name].start()

    z_info = Exchange(NZ, z, z_device, lambda t: msg.at[t], in_info, z_send.at[0], z_recv.at[0])
    z_cur = Exchange(NZ, z, z_device, lambda t: msg_cur.at[t], in_cur, z_send.at[1], z_recv.at[1])
    z_rep = Exchange(NZ, z, z_device, lambda t: rep_c.at[t], rep_d, z_send.at[2], z_recv.at[2])
    z_tree = Exchange(NZ, z, z_device, lambda t: crow, in_c, z_send.at[3], z_recv.at[3])
    j_info = Exchange(NJ, j, j_device, lambda t: mid_info, all_info, j_send.at[0], j_recv.at[0])
    j_cur = Exchange(NJ, j, j_device, lambda t: mid_cur.at[t], all_cur, j_send.at[1], j_recv.at[1])
    j_own = Exchange(NJ, j, j_device, lambda t: own_rows, near_rows, j_send.at[2], j_recv.at[2])
    j_tree = Exchange(NJ, j, j_device, lambda t: mid_c, all_c, j_send.at[3], j_recv.at[3])

    def pair_copy(number, src, dst, device):
        return pltpu.make_async_remote_copy(
            src_ref=src,
            dst_ref=dst,
            send_sem=p_send.at[number],
            recv_sem=p_recv.at[number],
            device_id=device,
            device_id_type=MESH,
        )

    other_core = (x, cell, 1 - c)
    lin_copy = pair_copy(0, lin_in, lins.at[c], other_core)
    tab_copy = pair_copy(1, tab_in, tabs.at[c], other_core)
    halo_right = pair_copy(2, win.at[pl.ds(LC, HW)], halo.at[0], g_device(1))
    halo_left = pair_copy(3, win.at[pl.ds(HW, HW)], halo.at[1], g_device(-1))
    x_right = pair_copy(4, up0.at[:, pl.ds(NCELL, 32)], xrows.at[0], x_device(1))
    x_left = pair_copy(5, up0.at[:, pl.ds(32, 32)], xrows.at[1], x_device(-1))

    loaded("pt")
    with jax.named_scope("pairs_out"):
        rows = [pt[f].astype(F32) for f in range(3)]
        rows = jnp.concatenate(rows + [jnp.zeros((CAP, LS), F32)], axis=0)
        columns = jnp.transpose(rows)
        lane = iota((LS, LS), 1)
        row_low = iota((LS, LS), 0) & (NJ - 1)
        info = jnp.zeros((LS, LS), F32)
        for slot in range(CAP):
            for field in range(2):
                hit = lane == row_low + (field * 32 + slot * NJ)
                info = info + jnp.where(hit, columns[:, 4 + 4 * field + slot][:, None], 0.0)
        spread = onehot((iota((NZ, LS), 1) >> 3) == iota((NZ, LS), 0))
        info = dot(spread, info.astype(BF16))
        for t in range(NZ):
            msg[t] = info[t : t + 1]
    loaded("cid", "vf", "con")
    with jax.named_scope("weighted"):
        ids = cid[...]
        scale = jnp.zeros((LC, VX), F32)
        for m in range(16):
            scale = jnp.where(ids == m, con[m], scale)
        win[pl.ds(HW, LC), :] = (vf[...].astype(F32) * scale).astype(BF16)
        own_rows[...] = win[pl.ds(pl.multiple_of(HW + c * HALF, 16), HALF), :]

    loaded("vrad", "cur", "srad", "host", "lout")
    with jax.named_scope("coarse"):
        weighted = win[pl.ds(HW, LC), :]
        outgoing = dot(weighted, vrad[...])
        surf_waves = dot(cur[...], srad[...])
        host_t = onehot(host[...] == iota((LC, LS), 0))
        leaf = lout[...]
        leaf_surf = dot(host_t, leaf, 0, 0)
        coarse = jnp.sum(leaf.astype(F32) * outgoing, axis=0, keepdims=True)
        coarse = coarse + jnp.sum(leaf_surf * surf_waves, axis=0, keepdims=True)
        crow[...] = coarse
    with jax.named_scope("currents_out"):
        own = cur[pl.ds(pl.multiple_of(c * 64, 64), 64), :]
        lane64 = iota((LS, 64), 1).astype(F32)
        parts = []
        for slot in range(CAP):
            pick = onehot(columns[:, slot : slot + 1] == lane64)
            parts.append(dot(pick, own).reshape(NZ, NJ, LS))
        msg_cur[...] = jnp.concatenate(parts, axis=1).astype(BF16)

    in_cur[pl.ds(z, 1)] = msg_cur[pl.ds(z, 1)]

    with jax.named_scope("barrier"):
        pl.semaphore_wait(barrier, (NZ - 1) + (NJ - 1) + 4)
    with jax.named_scope("start_j_own"):
        j_own.start_each(own_sem)
    with jax.named_scope("start_z_info"):
        z_info.start()
    in_info[pl.ds(z, 1)] = msg[pl.ds(z, 1)]
    near_rows[pl.ds(j, 1)] = own_rows[...][None]

    with jax.named_scope("start_z_tree"):
        z_tree.start()
        halo_right.start()
        halo_left.start()
        lin_copy.start()
        tab_copy.start()
    in_c[pl.ds(z, 1)] = crow[...][None]

    with jax.named_scope("start_z_cur"):
        z_cur.start()

    loaded("sv")
    with jax.named_scope("reply_table"):

        def fill(owner, rows):
            for kind in range(KINDS):
                block = dot(rows, sv[kind], 1, 1).astype(BF16)
                table[pl.ds(owner, 1), pl.ds(kind * HALF, HALF), :] = block[None]

        fill(j, own_rows[...])
        for step in range(1, NJ):
            owner = j_own.wait_one(own_sem, step)
            fill(owner, near_rows[pl.ds(owner, 1)].reshape(HALF, VX))
    with jax.named_scope("wait_z_info"):
        z_info.wait_recv()
    for t in range(NZ):
        mid_info[pl.ds(t, 1), :] = in_info[t]
    with jax.named_scope("start_j_info"):
        j_info.start()
    all_info[pl.ds(j, 1)] = mid_info[...][None]
    with jax.named_scope("wait_z_tree"):
        z_tree.wait_recv()
    for t in range(NZ):
        mid_c[pl.ds(t, 1), :] = in_c[t]
    j_tree.start()
    all_c[pl.ds(j, 1)] = mid_c[...][None]
    with jax.named_scope("replies"):
        lane384 = iota((NZ, KINDS * HALF), 1).astype(F32)
        codes = mid_info[...]
        codes = codes + HALF * pltpu.roll(codes, LS - 32, 1)
        for jj in range(NJ):
            picks = []
            for slot in range(CAP):
                at = slot * NJ + jj
                picks.append(jnp.where(codes[:, at : at + 1] == lane384, 1.0, 0.0))
            pick = jnp.concatenate(picks, axis=0).astype(BF16)
            f_rows[pl.ds(jj * 64, 64), :] = dot(pick, table[jj])
    with jax.named_scope("regroup_replies"):
        for zz in range(NZ):
            blocks = [f_rows[pl.ds(slot * NZ + zz, NJ, stride=64), :] for slot in range(CAP)]
            rep_c[zz] = jnp.concatenate(blocks, axis=0).astype(BF16)
    with jax.named_scope("start_z_rep"):
        z_rep.start()
    rep_d[pl.ds(z, 1)] = rep_c[pl.ds(z, 1)]

    with jax.named_scope("wait_z_cur"):
        z_cur.wait_recv()
    with jax.named_scope("regroup_currents"):
        f_rows[...] = in_cur[...].astype(F32).reshape(NZ * 32, LS)
        for jj in range(NJ):
            for slot in range(CAP):
                block = f_rows[pl.ds(slot * NJ + jj, NZ, stride=32), :]
                mid_cur[jj, slot] = block.astype(BF16)
    j_cur.start()
    all_cur[pl.ds(j, 1)] = mid_cur[pl.ds(j, 1)]

    with jax.named_scope("wait_halo"):
        halo_right.wait_recv()
        halo_left.wait_recv()
        loaded("near", "nb")
    with jax.named_scope("near"):
        first = jnp.where(g > 0, 1.0, 0.0)
        last = jnp.where(g < NX * NCELL - 1, 1.0, 0.0)
        win[pl.ds(0, HW), :] = jnp.where(first > 0.5, halo[0].astype(F32), 0.0).astype(BF16)
        win[pl.ds(HW + LC, HW), :] = jnp.where(last > 0.5, halo[1].astype(F32), 0.0).astype(BF16)
        win[pl.ds(2 * HW + LC, WIN - 2 * HW - LC), :] = jnp.zeros((WIN - 2 * HW - LC, VX), BF16)
        idx_pad[...] = jnp.zeros((32, 128), F32)
        idx_pad[pl.ds(0, NN), pl.ds(0, HALF)] = near_t[...].astype(F32)
        slots = jnp.transpose(idx_pad[...])[:HALF]
        lane_w = iota((HALF, WIN), 1).astype(F32)
        window = win[...]
        for n in range(NN):
            pick = onehot(slots[:, n : n + 1] == lane_w)
            gathered[n] = dot(pick, window).astype(BF16)

    with jax.named_scope("wait_j_tree"):
        j_tree.wait_recv()
    with jax.named_scope("section_rows"):
        for yy in range(NY):
            for cc in range(2):
                up0[cc, pl.ds(32 + yy, NZ, stride=NY), :] = all_c[2 * yy + cc]
    x_right.start()
    x_left.start()

    with jax.named_scope("near_blocks"):
        near = jnp.zeros((HALF, VX), F32)
        for n in range(NN):
            near = near + dot(gathered[n], nb[n])

    with jax.named_scope("wait_j_cur"):
        j_cur.wait_recv()
    with jax.named_scope("wait_j_info"):
        j_info.wait_recv()
    with jax.named_scope("coupled_volume"):
        codes = pltpu.roll(all_info[...].reshape(LS, LS), lax.rem(LS - j, LS), 1)
        lane384 = iota((LS, KINDS * HALF), 1).astype(F32)
        picks = []
        for slot in range(CAP):
            at = slot * NJ
            code = codes[:, at : at + 1] + HALF * codes[:, 32 + at : 33 + at]
            picks.append(onehot(code == lane384))
        sums = jnp.zeros((KINDS * HALF, LS), F32)
        for slot in range(CAP):
            sums = sums + dot(picks[slot], all_cur[:, slot].reshape(LS, LS), 0, 0)
        high = sums.astype(BF16)
        low = (sums - high.astype(F32)).astype(BF16)
        coupled = jnp.zeros((HALF, VX), F32)
        for kind in range(KINDS):
            part = slice(kind * HALF, (kind + 1) * HALF)
            coupled = coupled + dot(high[part], sv[kind]) + dot(low[part], sv[kind])

    with jax.named_scope("wait_x"):
        x_right.wait_recv()
        x_left.wait_recv()
    loaded("tab")
    tab_copy.wait_recv()
    with jax.named_scope("tree"):
        up0[:, pl.ds(0, 32), :] = jnp.where(x > 0, xrows[0], 0.0)
        up0[:, pl.ds(96, 32), :] = jnp.where(x < NX - 1, xrows[1], 0.0)
        ups = [up0, up1, up2, up3]
        waves = []
        for h in range(2):

            def entry(level, number):
                return tabs[h, level, pl.ds(number, 1), :]

            for level in range(3):
                count = 64 >> level
                even = ups[level][h, pl.ds(0, count, stride=2), :]
                odd = ups[level][h, pl.ds(1, count, stride=2), :]
                ups[level + 1][h] = entry(level, 4) * even + entry(level, 5) * odd
            terms = []
            for level in range(4):
                at = (32 + cell) >> level
                is_odd = (at & 1) == 1

                def row(offset):
                    return ups[level][h, pl.ds(at + offset, 1), :]

                term = jnp.where(is_odd, entry(level, 0) * row(-3), 0.0)
                term = term + entry(level, 1) * row(-2)
                term = term + entry(level, 2) * row(2)
                term = term + jnp.where(is_odd, 0.0, entry(level, 3) * row(3))
                terms.append(term)
            down = terms[3]
            for level in (2, 1, 0):
                is_odd = (((32 + cell) >> level) & 1) == 1
                down = terms[level] + jnp.where(is_odd, entry(level, 7), entry(level, 6)) * down
            waves.append(down)

    loaded("lin", "vrec", "srec")
    lin_copy.wait_recv()
    with jax.named_scope("far"):
        far_volume = jnp.zeros((HALF, VX), F32)
        far_surface = jnp.zeros((64, LS), F32)
        for h in range(2):
            wave = waves[h]
            leaf_own = lins[h, pl.ds(pl.multiple_of(c * HALF, 32), HALF), :].astype(F32)
            incoming = (leaf_own * wave).astype(BF16)
            far_volume = far_volume + dot(incoming, vrec[pl.ds(h * KH, KH), :])
            leaf_all = dot(host_t, lins[h], 0, 0)
            leaf_here = jnp.where(c == 0, leaf_all[:64], leaf_all[64:])
            incoming = (leaf_here * wave).astype(BF16)
            far_surface = far_surface + dot(incoming, srec[pl.ds(h * KH, KH), :])
    with jax.named_scope("volume_out"):
        field = vf[pl.ds(pl.multiple_of(c * HALF, 32), HALF), :].astype(F32)
        vout[...] = field + near + far_volume + coupled

    with jax.named_scope("wait_sends"):
        for exchange in (z_info, z_cur, z_tree, j_info, j_cur, j_own, j_tree):
            exchange.wait_send()
        for copy in (lin_copy, tab_copy, halo_right, halo_left, x_right, x_left):
            copy.wait_send()
    with jax.named_scope("wait_z_rep"):
        z_rep.wait_recv()
    with jax.named_scope("coupled_surface"):
        back = rep_d[...].astype(F32)
        sublane64 = iota((64, LS), 0)
        total = far_surface
        for slot in range(CAP):
            pick = onehot(pt[0, pl.ds(slot, 1), :] == sublane64)
            mine = back[:, slot * NJ : (slot + 1) * NJ, :].reshape(LS, LS).astype(BF16)
            total = total + dot(pick, mine)
        sout[...] = total

    z_rep.wait_send()


def on_device(
    volume_field, contrast_id, contrast, near_index, near_blocks, vol_radiation, surf_radiation,
    vol_receive, surf_receive, surface_current, surf_host, leaf_out, leaf_in, level_tables,
    sv_blocks, pair_table,
):
    inputs = (
        volume_field, contrast_id, contrast, near_index.T, near_blocks, vol_radiation,
        surf_radiation, vol_receive, surf_receive, surface_current, surf_host.reshape(1, LS),
        leaf_out, leaf_in, level_tables, sv_blocks, jnp.transpose(pair_table, (2, 1, 0)),
    )
    hbm = pl.BlockSpec(memory_space=pltpu.HBM)
    vmem = pl.BlockSpec(memory_space=pltpu.VMEM)
    specs = [hbm] * 16
    shapes = (jax.ShapeDtypeStruct((HALF, VX), F32), jax.ShapeDtypeStruct((64, LS), F32))
    return pl.pallas_call(
        kernel,
        out_shape=shapes,
        in_specs=specs,
        out_specs=(vmem, vmem),
        scratch_shapes=[
            pltpu.VMEM((LC, VX), BF16),
            pltpu.VMEM((LC, VX), jnp.int32),
            pltpu.SMEM((16,), F32),
            pltpu.VMEM((NN, HALF), jnp.int32),
            pltpu.VMEM((NN, VX, VX), BF16),
            pltpu.VMEM((VX, KH), BF16),
            pltpu.VMEM((LS, KH), BF16),
            pltpu.VMEM((2 * KH, VX), BF16),
            pltpu.VMEM((2 * KH, LS), BF16),
            pltpu.VMEM((LS, LS), BF16),
            pltpu.VMEM((1, LS), jnp.int32),
            pltpu.VMEM((LC, KH), BF16),
            pltpu.VMEM((KINDS, LS, VX), BF16),
            pltpu.VMEM((3, CAP, LS), jnp.int32),
            pltpu.VMEM((WIN, VX), BF16),
            pltpu.VMEM((2, HW, VX), BF16),
            pltpu.VMEM((NZ, 1, LS), F32),
            pltpu.VMEM((NZ, 1, LS), F32),
            pltpu.VMEM((NZ, LS), F32),
            pltpu.VMEM((NJ, NZ, LS), F32),
            pltpu.VMEM((1, KH), F32),
            pltpu.VMEM((NZ, 1, KH), F32),
            pltpu.VMEM((NZ, KH), F32),
            pltpu.VMEM((NJ, NZ, KH), F32),
            pltpu.VMEM((NZ, 32, LS), BF16),
            pltpu.VMEM((NZ, 32, LS), BF16),
            pltpu.VMEM((512, LS), F32),
            pltpu.VMEM((NJ, CAP, NZ, LS), BF16),
            pltpu.VMEM((NJ, CAP, NZ, LS), BF16),
            pltpu.VMEM((NJ, KINDS * HALF, LS), BF16),
            pltpu.VMEM((HALF, VX), BF16),
            pltpu.VMEM((NJ, HALF, VX), BF16),
            pltpu.VMEM((NZ, 32, LS), BF16),
            pltpu.VMEM((NZ, 32, LS), BF16),
            pltpu.VMEM((2, 128, KH), F32),
            pltpu.VMEM((2, 2, 32, KH), F32),
            pltpu.VMEM((2, 64, KH), F32),
            pltpu.VMEM((2, 32, KH), F32),
            pltpu.VMEM((2, 16, KH), F32),
            pltpu.VMEM((2, LC, KH), BF16),
            pltpu.VMEM((2, 4, 8, KH), F32),
            pltpu.VMEM((32, 128), F32),
            pltpu.VMEM((NN, HALF, VX), BF16),
            pltpu.SemaphoreType.DMA((4,)),
            pltpu.SemaphoreType.DMA((4,)),
            pltpu.SemaphoreType.DMA((4,)),
            pltpu.SemaphoreType.DMA((4,)),
            pltpu.SemaphoreType.DMA((6,)),
            pltpu.SemaphoreType.DMA((6,)),
            pltpu.SemaphoreType.DMA((NJ,)),
            pltpu.SemaphoreType.DMA((16,)),
        ],
        compiler_params=pltpu.CompilerParams(
            collective_id=0, has_side_effects=True, vmem_limit_bytes=40 * 1024 * 1024
        ),
    )(*[pltpu.with_memory_space_constraint(array, pltpu.HBM) for array in inputs])


def solution(mesh):
    in_specs = (
        P(("sec", "cell"), None),
        P(("sec", "cell"), None),
        P(),
        P(("sec", "cell", "dir"), None),
        P(),
        P(None, "dir"),
        P(None, "dir"),
        P(),
        P(),
        P(("sec", "cell"), None),
        P(("sec", "cell")),
        P(None, "dir"),
        P(None, "dir"),
        P(None, None, "dir"),
        P(),
        P(("sec", "cell", "dir"), None, None),
    )
    out_specs = (P(("sec", "cell", "dir"), None), P(("sec", "cell", "dir"), None))
    return jax.shard_map(
        on_device, mesh=mesh, in_specs=in_specs, out_specs=out_specs, check_vma=False
    )
```

```python
import jax
import jax.numpy as jnp
from jax import lax
from jax.experimental import pallas as pl
from jax.experimental.pallas import tpu as pltpu
from jax.sharding import PartitionSpec as P

MESH = pl.DeviceIdType.MESH
F32 = jnp.float32
BF16 = jnp.bfloat16

NX = 4
NZ = 16
NY = 4
NJ = 8
NCELL = NZ * NY
CAP = 4
KINDS = 4
LC = 192
HALF = 96
LS = 128
HW = 48
NN = 27
VX = 256
KH = 128
WIN = 384


def dot(a, b, ca=1, cb=0):
    return lax.dot_general(a, b, (((ca,), (cb,)), ((), ())), preferred_element_type=F32)


def onehot(mask):
    return jnp.where(mask, 1.0, 0.0).astype(BF16)


def iota(shape, dim):
    return lax.broadcasted_iota(jnp.int32, shape, dim)


class Exchange:
    def __init__(self, count, me, device, src, dst, send, recv):
        self.count, self.me, self.device = count, me, device
        self.src, self.dst, self.send, self.recv = src, dst, send, recv

    def start(self):
        def body(step, carry):
            low = lax.div(self.count + 1 - step, 2)
            offset = jnp.where(lax.rem(step, 2) == 1, low, self.count - low)
            target = lax.rem(self.me + offset, self.count)
            pltpu.make_async_remote_copy(
                src_ref=self.src(target),
                dst_ref=self.dst.at[self.me],
                send_sem=self.send,
                recv_sem=self.recv,
                device_id=self.device(target),
                device_id_type=MESH,
            ).start()
            return carry

        lax.fori_loop(1, self.count, body, 0)

    def offset(self, step):
        low = (self.count + 1 - step) // 2
        return low if step % 2 == 1 else self.count - low

    def start_each(self, recv):
        for step in range(1, self.count):
            target = lax.rem(self.me + self.offset(step), self.count)
            pltpu.make_async_remote_copy(
                src_ref=self.src(target),
                dst_ref=self.dst.at[self.me],
                send_sem=self.send,
                recv_sem=recv.at[step],
                device_id=self.device(target),
                device_id_type=MESH,
            ).start()

    def wait_one(self, recv, step):
        source = lax.rem(self.me + self.count - self.offset(step), self.count)
        pltpu.make_async_remote_copy(
            src_ref=self.dst.at[source],
            dst_ref=self.dst.at[source],
            send_sem=self.send,
            recv_sem=recv.at[step],
            device_id=self.device(source),
            device_id_type=MESH,
        ).wait_recv()
        return source

    def all_blocks(self):
        blocks = self.dst.at[pl.ds(0, self.count - 1)]
        return pltpu.make_async_remote_copy(
            src_ref=blocks,
            dst_ref=blocks,
            send_sem=self.send,
            recv_sem=self.recv,
            device_id=self.device(lax.rem(self.me + 1, self.count)),
            device_id_type=MESH,
        )

    def wait_recv(self):
        self.all_blocks().wait_recv()

    def wait_send(self):
        self.all_blocks().wait_send()


def kernel(
    vf_in, cid_in, con_in, near_in, nb_in, vrad_in, srad_in, vrec_in, srec_in, cur_in, host_in,
    lout_in, lin_in, tab_in, sv_in, pt_in,
    vout, sout,
    vf, cid, con, near_t, nb, vrad, srad, vrec, srec, cur, host, lout, sv, pt, win, halo, msg, in_info, mid_info, all_info, crow, in_c, mid_c, all_c,
    msg_cur, in_cur, f_rows, mid_cur, all_cur,
    table, own_rows, near_rows, rep_c, rep_d,
    up0, xrows, up1, up2, up3,
    lins, tabs, idx_pad, gathered,
    z_send, z_recv, j_send, j_recv, p_send, p_recv, own_sem, load_sem,
):
    x = lax.axis_index("sec")
    cell = lax.axis_index("cell")
    c = lax.axis_index("dir")
    z = lax.div(cell, NY)
    y = lax.rem(cell, NY)
    j = y * 2 + c
    g = x * NCELL + cell

    loads = {}
    order = [
        ("pt", pt_in, pt), ("cur", cur_in, cur), ("cid", cid_in, cid), ("vf", vf_in, vf),
        ("con", con_in, con), ("vrad", vrad_in, vrad), ("srad", srad_in, srad),
        ("host", host_in, host), ("lout", lout_in, lout), ("sv", sv_in, sv),
        ("near", near_in, near_t), ("lin", lin_in, lins.at[c]), ("tab", tab_in, tabs.at[c]),
        ("nb", nb_in, nb), ("vrec", vrec_in, vrec), ("srec", srec_in, srec),
    ]
    for number, (name, src, dst) in enumerate(order):
        loads[name] = pltpu.make_async_copy(src, dst, load_sem.at[number])
    loads["pt"].start()

    def loaded(*names):
        for name in names:
            loads[name].wait()

    def z_device(other):
        return (x, other * NY + y, c)

    def j_device(other):
        return (x, z * NY + lax.div(other, 2), lax.rem(other, 2))

    def g_device(step):
        other = lax.rem(g + step + NX * NCELL, NX * NCELL)
        return (lax.div(other, NCELL), lax.rem(other, NCELL), c)

    def x_device(step):
        return (lax.rem(x + step + NX, NX), cell, c)

    barrier = pltpu.get_barrier_semaphore()

    def greet(device):
        pl.semaphore_signal(barrier, inc=1, device_id=device, device_id_type=MESH)

    def greet_z(step, carry):
        greet(z_device(lax.rem(z + step, NZ)))
        return carry

    def greet_j(step, carry):
        greet(j_device(lax.rem(j + step, NJ)))
        return carry

    lax.fori_loop(1, NZ, greet_z, 0)
    lax.fori_loop(1, NJ, greet_j, 0)
    for step in (-1, 1):
        greet(g_device(step))
        greet(x_device(step))
    for name in loads:
        if name != "pt":
            loads[name].start()

    z_info = Exchange(NZ, z, z_device, lambda t: msg.at[t], in_info, z_send.at[0], z_recv.at[0])
    z_cur = Exchange(NZ, z, z_device, lambda t: msg_cur.at[t], in_cur, z_send.at[1], z_recv.at[1])
    z_rep = Exchange(NZ, z, z_device, lambda t: rep_c.at[t], rep_d, z_send.at[2], z_recv.at[2])
    z_tree = Exchange(NZ, z, z_device, lambda t: crow, in_c, z_send.at[3], z_recv.at[3])
    j_info = Exchange(NJ, j, j_device, lambda t: mid_info, all_info, j_send.at[0], j_recv.at[0])
    j_cur = Exchange(NJ, j, j_device, lambda t: mid_cur.at[t], all_cur, j_send.at[1], j_recv.at[1])
    j_own = Exchange(NJ, j, j_device, lambda t: own_rows, near_rows, j_send.at[2], j_recv.at[2])
    j_tree = Exchange(NJ, j, j_device, lambda t: mid_c, all_c, j_send.at[3], j_recv.at[3])

    def pair_copy(number, src, dst, device):
        return pltpu.make_async_remote_copy(
            src_ref=src,
            dst_ref=dst,
            send_sem=p_send.at[number],
            recv_sem=p_recv.at[number],
            device_id=device,
            device_id_type=MESH,
        )

    other_core = (x, cell, 1 - c)
    lin_copy = pair_copy(0, lin_in, lins.at[c], other_core)
    tab_copy = pair_copy(1, tab_in, tabs.at[c], other_core)
    halo_right = pair_copy(2, win.at[pl.ds(LC, HW)], halo.at[0], g_device(1))
    halo_left = pair_copy(3, win.at[pl.ds(HW, HW)], halo.at[1], g_device(-1))
    x_right = pair_copy(4, up0.at[:, pl.ds(NCELL, 32)], xrows.at[0], x_device(1))
    x_left = pair_copy(5, up0.at[:, pl.ds(32, 32)], xrows.at[1], x_device(-1))

    loaded("pt")
    with jax.named_scope("pairs_out"):
        rows = [pt[f].astype(F32) for f in range(3)]
        rows = jnp.concatenate(rows + [jnp.zeros((CAP, LS), F32)], axis=0)
        columns = jnp.transpose(rows)
        lane = iota((LS, LS), 1)
        row_low = iota((LS, LS), 0) & (NJ - 1)
        info = jnp.zeros((LS, LS), F32)
        for slot in range(CAP):
            for field in range(2):
                hit = lane == row_low + (field * 32 + slot * NJ)
                info = info + jnp.where(hit, columns[:, 4 + 4 * field + slot][:, None], 0.0)
        spread = onehot((iota((NZ, LS), 1) >> 3) == iota((NZ, LS), 0))
        info = dot(spread, info.astype(BF16))
        for t in range(NZ):
            msg[t] = info[t : t + 1]
    loaded("cid", "vf", "con")
    with jax.named_scope("weighted"):
        ids = cid[...]
        scale = jnp.zeros((LC, VX), F32)
        for m in range(16):
            scale = jnp.where(ids == m, con[m], scale)
        win[pl.ds(HW, LC), :] = (vf[...].astype(F32) * scale).astype(BF16)
        own_rows[...] = win[pl.ds(pl.multiple_of(HW + c * HALF, 16), HALF), :]

    loaded("vrad", "cur", "srad", "host", "lout")
    with jax.named_scope("coarse"):
        weighted = win[pl.ds(HW, LC), :]
        outgoing = dot(weighted, vrad[...])
        surf_waves = dot(cur[...], srad[...])
        host_t = onehot(host[...] == iota((LC, LS), 0))
        leaf = lout[...]
        leaf_surf = dot(host_t, leaf, 0, 0)
        coarse = jnp.sum(leaf.astype(F32) * outgoing, axis=0, keepdims=True)
        coarse = coarse + jnp.sum(leaf_surf * surf_waves, axis=0, keepdims=True)
        crow[...] = coarse
    with jax.named_scope("currents_out"):
        own = cur[pl.ds(pl.multiple_of(c * 64, 64), 64), :]
        lane64 = iota((LS, 64), 1).astype(F32)
        parts = []
        for slot in range(CAP):
            pick = onehot(columns[:, slot : slot + 1] == lane64)
            parts.append(dot(pick, own).reshape(NZ, NJ, LS))
        msg_cur[...] = jnp.concatenate(parts, axis=1).astype(BF16)

    in_cur[pl.ds(z, 1)] = msg_cur[pl.ds(z, 1)]

    with jax.named_scope("barrier"):
        pl.semaphore_wait(barrier, (NZ - 1) + (NJ - 1) + 4)
    with jax.named_scope("start_j_own"):
        j_own.start_each(own_sem)
    with jax.named_scope("start_z_info"):
        z_info.start()
    in_info[pl.ds(z, 1)] = msg[pl.ds(z, 1)]
    near_rows[pl.ds(j, 1)] = own_rows[...][None]

    with jax.named_scope("start_z_tree"):
        z_tree.start()
    in_c[pl.ds(z, 1)] = crow[...][None]

    with jax.named_scope("start_z_cur"):
        z_cur.start()
        halo_right.start()
        halo_left.start()
        lin_copy.start()
        tab_copy.start()

    loaded("sv")
    with jax.named_scope("reply_table"):

        def fill(owner, rows):
            for kind in range(KINDS):
                block = dot(rows, sv[kind], 1, 1).astype(BF16)
                table[pl.ds(owner, 1), pl.ds(kind * HALF, HALF), :] = block[None]

        fill(j, own_rows[...])
        for step in range(1, NJ):
            owner = j_own.wait_one(own_sem, step)
            fill(owner, near_rows[pl.ds(owner, 1)].reshape(HALF, VX))
    with jax.named_scope("wait_z_info"):
        z_info.wait_recv()
    for t in range(NZ):
        mid_info[pl.ds(t, 1), :] = in_info[t]
    with jax.named_scope("start_j_info"):
        j_info.start()
    all_info[pl.ds(j, 1)] = mid_info[...][None]
    with jax.named_scope("wait_z_tree"):
        z_tree.wait_recv()
    for t in range(NZ):
        mid_c[pl.ds(t, 1), :] = in_c[t]
    j_tree.start()
    all_c[pl.ds(j, 1)] = mid_c[...][None]
    with jax.named_scope("replies"):
        lane384 = iota((NZ, KINDS * HALF), 1).astype(F32)
        codes = mid_info[...]
        codes = codes + HALF * pltpu.roll(codes, LS - 32, 1)
        for jj in range(NJ):
            picks = []
            for slot in range(CAP):
                at = slot * NJ + jj
                picks.append(jnp.where(codes[:, at : at + 1] == lane384, 1.0, 0.0))
            pick = jnp.concatenate(picks, axis=0).astype(BF16)
            f_rows[pl.ds(jj * 64, 64), :] = dot(pick, table[jj])
    with jax.named_scope("regroup_replies"):
        for zz in range(NZ):
            blocks = [f_rows[pl.ds(slot * NZ + zz, NJ, stride=64), :] for slot in range(CAP)]
            rep_c[zz] = jnp.concatenate(blocks, axis=0).astype(BF16)
    with jax.named_scope("start_z_rep"):
        z_rep.start()
    rep_d[pl.ds(z, 1)] = rep_c[pl.ds(z, 1)]

    with jax.named_scope("wait_z_cur"):
        z_cur.wait_recv()
    with jax.named_scope("regroup_currents"):
        f_rows[...] = in_cur[...].astype(F32).reshape(NZ * 32, LS)
        for jj in range(NJ):
            for slot in range(CAP):
                block = f_rows[pl.ds(slot * NJ + jj, NZ, stride=32), :]
                mid_cur[jj, slot] = block.astype(BF16)
    j_cur.start()
    all_cur[pl.ds(j, 1)] = mid_cur[pl.ds(j, 1)]

    with jax.named_scope("wait_halo"):
        halo_right.wait_recv()
        halo_left.wait_recv()
        loaded("near", "nb")
    with jax.named_scope("near"):
        first = jnp.where(g > 0, 1.0, 0.0)
        last = jnp.where(g < NX * NCELL - 1, 1.0, 0.0)
        win[pl.ds(0, HW), :] = jnp.where(first > 0.5, halo[0].astype(F32), 0.0).astype(BF16)
        win[pl.ds(HW + LC, HW), :] = jnp.where(last > 0.5, halo[1].astype(F32), 0.0).astype(BF16)
        win[pl.ds(2 * HW + LC, WIN - 2 * HW - LC), :] = jnp.zeros((WIN - 2 * HW - LC, VX), BF16)
        idx_pad[...] = jnp.zeros((32, 128), F32)
        idx_pad[pl.ds(0, NN), pl.ds(0, HALF)] = near_t[...].astype(F32)
        slots = jnp.transpose(idx_pad[...])[:HALF]
        lane_w = iota((HALF, WIN), 1).astype(F32)
        window = win[...]
        for n in range(NN):
            pick = onehot(slots[:, n : n + 1] == lane_w)
            gathered[n] = dot(pick, window).astype(BF16)

    with jax.named_scope("wait_j_tree"):
        j_tree.wait_recv()
    with jax.named_scope("section_rows"):
        for yy in range(NY):
            for cc in range(2):
                up0[cc, pl.ds(32 + yy, NZ, stride=NY), :] = all_c[2 * yy + cc]
    x_right.start()
    x_left.start()

    with jax.named_scope("near_blocks"):
        near = jnp.zeros((HALF, VX), F32)
        for n in range(NN):
            near = near + dot(gathered[n], nb[n])

    with jax.named_scope("wait_j_cur"):
        j_cur.wait_recv()
    with jax.named_scope("wait_j_info"):
        j_info.wait_recv()
    with jax.named_scope("coupled_volume"):
        codes = pltpu.roll(all_info[...].reshape(LS, LS), lax.rem(LS - j, LS), 1)
        lane384 = iota((LS, KINDS * HALF), 1).astype(F32)
        picks = []
        for slot in range(CAP):
            at = slot * NJ
            code = codes[:, at : at + 1] + HALF * codes[:, 32 + at : 33 + at]
            picks.append(onehot(code == lane384))
        sums = jnp.zeros((KINDS * HALF, LS), F32)
        for slot in range(CAP):
            sums = sums + dot(picks[slot], all_cur[:, slot].reshape(LS, LS), 0, 0)
        high = sums.astype(BF16)
        low = (sums - high.astype(F32)).astype(BF16)
        coupled = jnp.zeros((HALF, VX), F32)
        for kind in range(KINDS):
            part = slice(kind * HALF, (kind + 1) * HALF)
            coupled = coupled + dot(high[part], sv[kind]) + dot(low[part], sv[kind])

    with jax.named_scope("wait_x"):
        x_right.wait_recv()
        x_left.wait_recv()
    loaded("tab")
    tab_copy.wait_recv()
    with jax.named_scope("tree"):
        up0[:, pl.ds(0, 32), :] = jnp.where(x > 0, xrows[0], 0.0)
        up0[:, pl.ds(96, 32), :] = jnp.where(x < NX - 1, xrows[1], 0.0)
        ups = [up0, up1, up2, up3]
        waves = []
        for h in range(2):

            def entry(level, number):
                return tabs[h, level, pl.ds(number, 1), :]

            for level in range(3):
                count = 64 >> level
                even = ups[level][h, pl.ds(0, count, stride=2), :]
                odd = ups[level][h, pl.ds(1, count, stride=2), :]
                ups[level + 1][h] = entry(level, 4) * even + entry(level, 5) * odd
            terms = []
            for level in range(4):
                at = (32 + cell) >> level
                is_odd = (at & 1) == 1

                def row(offset):
                    return ups[level][h, pl.ds(at + offset, 1), :]

                term = jnp.where(is_odd, entry(level, 0) * row(-3), 0.0)
                term = term + entry(level, 1) * row(-2)
                term = term + entry(level, 2) * row(2)
                term = term + jnp.where(is_odd, 0.0, entry(level, 3) * row(3))
                terms.append(term)
            down = terms[3]
            for level in (2, 1, 0):
                is_odd = (((32 + cell) >> level) & 1) == 1
                down = terms[level] + jnp.where(is_odd, entry(level, 7), entry(level, 6)) * down
            waves.append(down)

    loaded("lin", "vrec", "srec")
    lin_copy.wait_recv()
    with jax.named_scope("far"):
        far_volume = jnp.zeros((HALF, VX), F32)
        far_surface = jnp.zeros((64, LS), F32)
        for h in range(2):
            wave = waves[h]
            leaf_own = lins[h, pl.ds(pl.multiple_of(c * HALF, 32), HALF), :].astype(F32)
            incoming = (leaf_own * wave).astype(BF16)
            far_volume = far_volume + dot(incoming, vrec[pl.ds(h * KH, KH), :])
            leaf_all = dot(host_t, lins[h], 0, 0)
            leaf_here = jnp.where(c == 0, leaf_all[:64], leaf_all[64:])
            incoming = (leaf_here * wave).astype(BF16)
            far_surface = far_surface + dot(incoming, srec[pl.ds(h * KH, KH), :])
    with jax.named_scope("volume_out"):
        field = vf[pl.ds(pl.multiple_of(c * HALF, 32), HALF), :].astype(F32)
        vout[...] = field + near + far_volume + coupled

    with jax.named_scope("wait_sends"):
        for exchange in (z_info, z_cur, z_tree, j_info, j_cur, j_own, j_tree):
            exchange.wait_send()
        for copy in (lin_copy, tab_copy, halo_right, halo_left, x_right, x_left):
            copy.wait_send()
    with jax.named_scope("wait_z_rep"):
        z_rep.wait_recv()
    with jax.named_scope("coupled_surface"):
        back = rep_d[...].astype(F32)
        sublane64 = iota((64, LS), 0)
        total = far_surface
        for slot in range(CAP):
            pick = onehot(pt[0, pl.ds(slot, 1), :] == sublane64)
            mine = back[:, slot * NJ : (slot + 1) * NJ, :].reshape(LS, LS).astype(BF16)
            total = total + dot(pick, mine)
        sout[...] = total

    z_rep.wait_send()


def on_device(
    volume_field, contrast_id, contrast, near_index, near_blocks, vol_radiation, surf_radiation,
    vol_receive, surf_receive, surface_current, surf_host, leaf_out, leaf_in, level_tables,
    sv_blocks, pair_table,
):
    inputs = (
        volume_field, contrast_id, contrast, near_index.T, near_blocks, vol_radiation,
        surf_radiation, vol_receive, surf_receive, surface_current, surf_host.reshape(1, LS),
        leaf_out, leaf_in, level_tables, sv_blocks, jnp.transpose(pair_table, (2, 1, 0)),
    )
    hbm = pl.BlockSpec(memory_space=pltpu.HBM)
    vmem = pl.BlockSpec(memory_space=pltpu.VMEM)
    specs = [hbm] * 16
    shapes = (jax.ShapeDtypeStruct((HALF, VX), F32), jax.ShapeDtypeStruct((64, LS), F32))
    return pl.pallas_call(
        kernel,
        out_shape=shapes,
        in_specs=specs,
        out_specs=(vmem, vmem),
        scratch_shapes=[
            pltpu.VMEM((LC, VX), BF16),
            pltpu.VMEM((LC, VX), jnp.int32),
            pltpu.SMEM((16,), F32),
            pltpu.VMEM((NN, HALF), jnp.int32),
            pltpu.VMEM((NN, VX, VX), BF16),
            pltpu.VMEM((VX, KH), BF16),
            pltpu.VMEM((LS, KH), BF16),
            pltpu.VMEM((2 * KH, VX), BF16),
            pltpu.VMEM((2 * KH, LS), BF16),
            pltpu.VMEM((LS, LS), BF16),
            pltpu.VMEM((1, LS), jnp.int32),
            pltpu.VMEM((LC, KH), BF16),
            pltpu.VMEM((KINDS, LS, VX), BF16),
            pltpu.VMEM((3, CAP, LS), jnp.int32),
            pltpu.VMEM((WIN, VX), BF16),
            pltpu.VMEM((2, HW, VX), BF16),
            pltpu.VMEM((NZ, 1, LS), F32),
            pltpu.VMEM((NZ, 1, LS), F32),
            pltpu.VMEM((NZ, LS), F32),
            pltpu.VMEM((NJ, NZ, LS), F32),
            pltpu.VMEM((1, KH), F32),
            pltpu.VMEM((NZ, 1, KH), F32),
            pltpu.VMEM((NZ, KH), F32),
            pltpu.VMEM((NJ, NZ, KH), F32),
            pltpu.VMEM((NZ, 32, LS), BF16),
            pltpu.VMEM((NZ, 32, LS), BF16),
            pltpu.VMEM((512, LS), F32),
            pltpu.VMEM((NJ, CAP, NZ, LS), BF16),
            pltpu.VMEM((NJ, CAP, NZ, LS), BF16),
            pltpu.VMEM((NJ, KINDS * HALF, LS), BF16),
            pltpu.VMEM((HALF, VX), BF16),
            pltpu.VMEM((NJ, HALF, VX), BF16),
            pltpu.VMEM((NZ, 32, LS), BF16),
            pltpu.VMEM((NZ, 32, LS), BF16),
            pltpu.VMEM((2, 128, KH), F32),
            pltpu.VMEM((2, 2, 32, KH), F32),
            pltpu.VMEM((2, 64, KH), F32),
            pltpu.VMEM((2, 32, KH), F32),
            pltpu.VMEM((2, 16, KH), F32),
            pltpu.VMEM((2, LC, KH), BF16),
            pltpu.VMEM((2, 4, 8, KH), F32),
            pltpu.VMEM((32, 128), F32),
            pltpu.VMEM((NN, HALF, VX), BF16),
            pltpu.SemaphoreType.DMA((4,)),
            pltpu.SemaphoreType.DMA((4,)),
            pltpu.SemaphoreType.DMA((4,)),
            pltpu.SemaphoreType.DMA((4,)),
            pltpu.SemaphoreType.DMA((6,)),
            pltpu.SemaphoreType.DMA((6,)),
            pltpu.SemaphoreType.DMA((NJ,)),
            pltpu.SemaphoreType.DMA((16,)),
        ],
        compiler_params=pltpu.CompilerParams(
            collective_id=0, has_side_effects=True, vmem_limit_bytes=40 * 1024 * 1024
        ),
    )(*[pltpu.with_memory_space_constraint(array, pltpu.HBM) for array in inputs])


def solution(mesh):
    in_specs = (
        P(("sec", "cell"), None),
        P(("sec", "cell"), None),
        P(),
        P(("sec", "cell", "dir"), None),
        P(),
        P(None, "dir"),
        P(None, "dir"),
        P(),
        P(),
        P(("sec", "cell"), None),
        P(("sec", "cell")),
        P(None, "dir"),
        P(None, "dir"),
        P(None, None, "dir"),
        P(),
        P(("sec", "cell", "dir"), None, None),
    )
    out_specs = (P(("sec", "cell", "dir"), None), P(("sec", "cell", "dir"), None))
    return jax.shard_map(
        on_device, mesh=mesh, in_specs=in_specs, out_specs=out_specs, check_vma=False
    )
```
